512 devices in a mesh: seq: 128 (over y, z, core), head: 4 (over x).
Axes of the slice: x: 4, y: 4, z: 16, core: 2. Of those that a mesh axis runs over, the one named last changes fastest.
Arguments:
- stream: bfloat16 [16384, 5120], P('seq'), may hold values from -24 to 24
- queries: bfloat16 [16384, 2560], P('seq', 'head'), as said below
- keys: bfloat16 [16384, 2560], P('seq', 'head'), as said below
- values: bfloat16 [16384, 2560], P('seq', 'head'), may hold values from -6 to 6
- router_weight: bfloat16 [5120], replicated, may hold values from -0.111328125 to 0.111328125
- chosen: int32 [2048], replicated, may hold values from 0 to 16383, as said below
- owner: int32 [2048], replicated, may hold values from 0 to 127, as said below
- grad_out: bfloat16 [2048, 2560], P('seq', 'head'), may hold values from -6 to 6
Outputs:
- block_out: bfloat16 [2048, 2560], P('seq', 'head')
- grad_queries: bfloat16 [2048, 2560], P('seq', 'head')
- grad_keys: bfloat16 [2048, 2560], P('seq', 'head')
- grad_values: bfloat16 [2048, 2560], P('seq', 'head')
- grad_router: float32 [5120], P('seq')
The draws below stay inside these ranges and needn't reach their ends.
Inputs may be any that keep to these rules, and one draw needn't show every extreme that they name: `chosen`: entries j * 16 to (j + 1) * 16 - 1 are distinct positions of tokens j * 128 to (j + 1) * 128 - 1, increasing. Every owner is named by exactly 16 rows. `queries`: entries lie between -240 and 240. `keys`: entries lie between -9 and 9.
All inputs are finite; a program needn't handle non-finite values.
Results may differ from the reference program's by a relative error of at most 0.017.
Values may be sent and summed in bfloat16 or wider, within the bound.
A program may use at most 64 MiB of HBM per device.

```python
import jax
import jax.numpy as jnp
from jax import lax

D = 5120
HEAD_DIM = 128
HEADS = 20
TOK_DEV = 128
CAP_DEV = 16
TOKENS = 16384
CHOSEN = 2048


def shared_rows(key):
    return jax.random.normal(key, (TOKENS, HEADS * HEAD_DIM), jnp.float32)


def draw_keys(key, part):
    shared = shared_rows(key)
    key = jax.random.fold_in(key, 11)
    jitter = jax.random.normal(key, shared.shape, jnp.float32)
    return (0.6 * shared + 0.8 * jitter).astype(jnp.bfloat16)


def draw_queries(key, part):
    shared = shared_rows(key)
    key = jax.random.fold_in(key, 7)
    result = 2.0 * jax.random.normal(key, shared.shape, jnp.float32)
    return result.astype(jnp.bfloat16)


def draw_chosen(key, part):
    key = jax.random.fold_in(key, 3)
    block_count = CHOSEN // CAP_DEV
    block_keys = jax.random.split(key, block_count)

    def block_pick(block_key):
        return jnp.sort(jax.random.permutation(block_key, TOK_DEV)[:CAP_DEV])
    picked = jax.vmap(block_pick)(block_keys)
    starts = jnp.arange(block_count, dtype=jnp.int32) * TOK_DEV
    return (picked.astype(jnp.int32) + starts[:, None]).reshape(-1).astype(jnp.int32)


def draw_owner(key, part):
    key = jax.random.fold_in(key, 5)
    return (jax.random.permutation(key, CHOSEN) // CAP_DEV).astype(jnp.int32)


def strengthened(array, key, source, target, shards_of, factor):
    owner, partner = [(jnp.arange(array.shape[axis_at]) // (array.shape[axis_at] // shards_of)).reshape([-1 if axis == axis_at else 1 for axis in range(array.ndim)]) for axis_at in (source, target)]
    chosen = jax.random.permutation(key, shards_of)[partner]
    strong = (owner == chosen) | (owner == (partner + shards_of // 2) % shards_of)
    return jnp.where(strong, factor * array, array)


def levels(stream_key, extent, pieces, least, largest):
    gain = 1.0
    for axis_at, blocks in pieces:
        draws = jax.random.uniform(jax.random.fold_in(jax.random.fold_in(stream_key, 6), axis_at), (blocks,), jnp.float32, least / len(pieces), largest / len(pieces))
        gain = gain * jnp.repeat(jnp.exp(draws), extent[axis_at] // blocks).reshape((-1,) + (1,) * (len(extent) - 1 - axis_at))
    return gain


def noise(rng, shape, spread, most, pieces=(), kind=jnp.bfloat16):
    values = spread * jax.random.normal(rng, shape, jnp.float32)
    if pieces:
        values = values * levels(rng, shape, pieces, -0.22, 0.18)
    return jnp.clip(values, -most, most).astype(kind)


def bell_draw_with(rng, dims, scale, limit, cuts, heavy, held_as=jnp.bfloat16):
    drawn = scale * jax.random.normal(rng, dims, jnp.float32)
    if cuts:
        drawn = drawn * levels(rng, dims, cuts, -0.22, 0.18)
    return jnp.clip(strengthened(drawn, jax.random.fold_in(rng, 3), *heavy), -limit, limit).astype(held_as)


def setup_inputs(seed: int = 0) -> dict:
    key_list = jax.random.split(jax.random.key(seed), 9)
    stream = bell_draw_with(key_list[0], (TOKENS, D), 1.0, 24.0, ((0, 128),), (0, 1, 128, 5.5))
    queries = draw_queries(jax.random.fold_in(key_list[8], 71), 0)
    keys = draw_keys(jax.random.fold_in(key_list[8], 71), 0)
    values = noise(key_list[3], (TOKENS, HEADS * HEAD_DIM), 1.0, 6.0, ((0, 128), (1, 4)))
    router_weight = noise(key_list[4], (D,), (2.0 / D ** 0.5), 0.111328125)
    chosen = draw_chosen(jax.random.fold_in(key_list[8], 71), 0)
    owner = draw_owner(jax.random.fold_in(key_list[8], 71), 0)
    grad_out = noise(key_list[7], (CHOSEN, HEADS * HEAD_DIM), 1.0, 6.0, ((0, 128), (1, 4)))
    return dict(stream=stream, queries=queries, keys=keys, values=values, router_weight=router_weight, chosen=chosen, owner=owner, grad_out=grad_out)


def head_terms(head_index, q_rows, k_rows, v_rows, ctx_grad, positions):
    column = head_index * HEAD_DIM
    q_head = lax.dynamic_slice_in_dim(q_rows, column, HEAD_DIM, 1)
    k_head = lax.dynamic_slice_in_dim(k_rows, column, HEAD_DIM, 1)
    v_head = lax.dynamic_slice_in_dim(v_rows, column, HEAD_DIM, 1)
    d_head = lax.dynamic_slice_in_dim(ctx_grad, column, HEAD_DIM, 1)
    head_scale = HEAD_DIM ** -0.5
    scores = jnp.dot(q_head, k_head.T, preferred_element_type=jnp.float32) * head_scale
    causal = positions[:, None] >= positions[None, :]
    scores = jnp.where(causal, scores, -jnp.inf)
    row_max = jnp.max(scores, axis=1, keepdims=True)
    log_total = row_max + jnp.log(jnp.sum(jnp.exp(scores - row_max), axis=1, keepdims=True))
    weights = jnp.exp(scores - log_total).astype(jnp.bfloat16)
    context = jnp.dot(weights, v_head, preferred_element_type=jnp.float32)
    row_delta = jnp.sum(d_head.astype(jnp.float32) * context, axis=1, keepdims=True)
    prob_grad = jnp.dot(d_head, v_head.T, preferred_element_type=jnp.float32)
    score_grad = (weights.astype(jnp.float32) * (prob_grad - row_delta)).astype(jnp.bfloat16)
    grad_q = jnp.dot(score_grad, k_head, preferred_element_type=jnp.float32) * head_scale
    grad_k = jnp.dot(score_grad.T, q_head, preferred_element_type=jnp.float32) * head_scale
    grad_v = jnp.dot(weights.T, d_head, preferred_element_type=jnp.float32)
    return context, grad_q, grad_k, grad_v


def merge_heads(stacked):
    return jnp.transpose(stacked, (1, 0, 2)).reshape(stacked.shape[1], HEADS * HEAD_DIM)


def reference(stream, queries, keys, values, router_weight, chosen, owner, grad_out):
    q_rows = jnp.take(queries, chosen, axis=0)
    k_rows = jnp.take(keys, chosen, axis=0)
    v_rows = jnp.take(values, chosen, axis=0)
    x_rows = jnp.take(stream, chosen, axis=0)
    router_logit = jnp.dot(x_rows, router_weight, preferred_element_type=jnp.float32).astype(jnp.bfloat16)
    gating = jax.nn.sigmoid(router_logit.astype(jnp.float32))
    slot_rows = jnp.argsort(owner, stable=True).astype(jnp.int32)
    upstream = jnp.zeros(grad_out.shape, jnp.float32).at[slot_rows].set(grad_out.astype(jnp.float32))
    ctx_grad = (gating[:, None] * upstream).astype(jnp.bfloat16)

    def one_head(head_index):
        return head_terms(head_index, q_rows, k_rows, v_rows, ctx_grad, chosen)

    context, grad_q, grad_k, grad_v = lax.map(one_head, jnp.arange(HEADS, dtype=jnp.int32))
    context = merge_heads(context)
    block_out = (gating[:, None] * context).astype(jnp.bfloat16)[slot_rows]
    gate_grad = jnp.sum(upstream * context, axis=1)
    logit_grad = gate_grad * gating * (1.0 - gating)
    grad_router = jnp.dot(logit_grad[None, :], x_rows.astype(jnp.float32), precision=lax.Precision.HIGHEST)[0]
    grad_queries = merge_heads(grad_q).astype(jnp.bfloat16)[slot_rows]
    grad_keys = merge_heads(grad_k).astype(jnp.bfloat16)[slot_rows]
    grad_values = merge_heads(grad_v).astype(jnp.bfloat16)[slot_rows]
    return (block_out, grad_queries, grad_keys, grad_values, grad_router)
```

```python
import jax
import jax.numpy as jnp
from jax import lax
from jax.experimental import pallas as pl
from jax.experimental.pallas import tpu as pltpu
from jax.sharding import PartitionSpec as P

NY, NZ, NX = 4, 16, 4
CAP = 16
HD = 128
ROWS = 2048
SCALE = HD**-0.5
MESH = pl.DeviceIdType.MESH
Q, K, G, V = 0, 1, 2, 3
F32, BF16 = jnp.float32, jnp.bfloat16


def dot(a, b, ca, cb):
    return lax.dot_general(a, b, (((ca,), (cb,)), ((), ())), preferred_element_type=F32)


def iota(shape, dim):
    return lax.broadcasted_iota(jnp.int32, shape, dim)


def kernel(
    chosen_ref, owner_ref, weight_ref, q_ref, k_ref, v_ref, g_ref, stream_ref,
    block_out_ref, gq_ref, gk_ref, gv_ref, router_ref,
    xs, pk, gat, xc, xt, ltile, lplane, lall, lsum,
    slot, pt, sel, ownx, st, wt, vt, gct, gc, rows, ob, outs,
    xg, gps, lgp, part, pr, fx,
    sem_x, p1s, p1r, ls, lr, rs, rr, fs, fr, dls, dlr, xts, xtr, outsem_s, outsem_r,
    xgs, xgr, gs, gr, prs, prr, fxs, fxr,
):
    seq, x = lax.axis_index("seq"), lax.axis_index("head")
    y, z, c = seq // 32, (seq // 2) % NZ, seq % 2
    me = y * 2 + c
    is_owner = (c == 0) | (y == 0)
    head = y * (1 - c) + 4 * c

    def dev(yy, zz, cc, xx):
        return (yy * 32 + zz * 2 + cc, xx)

    def remote(src, dst, ss, rsem, target):
        return pltpu.make_async_remote_copy(
            src_ref=src, dst_ref=dst, send_sem=ss, recv_sem=rsem, device_id=target, device_id_type=MESH
        )

    stream_copy = pltpu.make_async_copy(stream_ref, xs, sem_x)
    stream_copy.start()
    xt[...] = jnp.zeros_like(xt)

    plane = []
    for i in range(1, 8):
        p = (me + i) % 8
        plane.append((p // 2, p % 2))
    peers = [dev(yy, z, cc, x) for yy, cc in plane]
    peers += [dev(y, (z + i) % NZ, c, x) for i in range(1, NZ)]
    peers += [dev(y, z, c, (x + i) % NX) for i in range(1, NX)]
    barrier = pltpu.get_barrier_semaphore()
    for p in peers:
        pl.semaphore_signal(barrier, inc=1, device_id=p, device_id_type=MESH)

    token = jnp.zeros((CAP, 128), jnp.int32)
    for r in range(CAP):
        token = jnp.where(iota((CAP, 128), 0) == r, chosen_ref[seq * CAP + r] - seq * 128, token)
    pick = (token == iota((CAP, 128), 1)).astype(BF16)
    pk[Q] = dot(pick, q_ref[...], 1, 0).astype(BF16)
    pk[K] = dot(pick, k_ref[...], 1, 0).astype(BF16)
    pk[V] = dot(pick, v_ref[...], 1, 0).astype(BF16)
    pk[G] = g_ref[...]

    pl.semaphore_wait(barrier, len(peers))

    my_rows = pl.ds(pl.multiple_of(c * CAP, CAP), CAP)

    def to_head(h, target):
        return remote(
            pk.at[:, :, pl.ds(h * HD, HD)], gat.at[:, y, z, my_rows, :], p1s.at[h], p1r.at[me], target
        )

    for h in range(4):
        here = (c == 0) & (y == h)

        @pl.when(jnp.logical_not(here))
        def _():
            to_head(h, dev(h, z, 0, x)).start()

        @pl.when(here)
        def _():
            gat[:, y, z, my_rows, :] = pk[:, :, h * HD : (h + 1) * HD]

    @pl.when(c == 0)
    def _():
        to_head(4, dev(y, z, 1, x)).start()

    @pl.when(c == 1)
    def _():
        gat[:, y, z, my_rows, :] = pk[:, :, 4 * HD : 5 * HD]

    stream_copy.wait()
    for t in range(5):
        cols = slice(t * 1024, (t + 1) * 1024)
        xc[:, cols] = dot(pick, xs[:, cols], 1, 0).astype(BF16)
    xc[:, 5120:] = jnp.zeros((CAP, 128), BF16)
    logit = jnp.sum(xc[:, :5120].astype(F32) * weight_ref[...].astype(F32), axis=1, keepdims=True)
    spread = jnp.where(
        iota((CAP, 128), 1) == (seq % 8) * CAP + iota((CAP, 128), 0), logit, jnp.zeros((), F32)
    )
    line = jnp.sum(spread, axis=0, keepdims=True)
    ltile[...] = jnp.where(iota((16, 128), 0) == seq // 8, line, jnp.zeros((), F32)).astype(BF16)

    def to_logit(h):
        return remote(ltile, lplane.at[me], ls.at[h], lr.at[me], dev(h, z, 0, x))

    for h in range(4):
        here = (c == 0) & (y == h)

        @pl.when(jnp.logical_not(here))
        def _():
            to_logit(h).start()

        @pl.when(here)
        def _():
            lplane[me] = ltile[...]

    def window(zz):
        return pl.ds(pl.multiple_of(x * 1280 + (zz * 80 // 128) * 128, 128), 256)

    xt_rows = pl.ds(pl.multiple_of(z * 32 + c * CAP, CAP), CAP)

    def ring_core0(a, s, d, ahead=0):
        zz = (z - s - ahead + 2 * NZ) % NZ if d == 0 else (z + s + ahead) % NZ
        ref = lall.at[zz] if a == 4 else gat.at[a, :, zz]
        to = (z + 1) % NZ if d == 0 else (z + NZ - 1) % NZ
        return remote(ref, ref, rs.at[d, a, s], rr.at[d, a, s], dev(y, to, c, x))

    def ring_core1(a, s, d, ahead=0):
        zz = (z - s - ahead + 2 * NZ) % NZ if d == 0 else (z + s + ahead) % NZ
        ref = gat.at[a, y, zz]
        to = (z + 1) % NZ if d == 0 else (z + NZ - 1) % NZ
        return remote(ref, ref, rs.at[d, a, s], rr.at[d, a, s], dev(y, to, c, x))

    def forward(zz, k):
        ref = gat.at[:, y, zz]
        return remote(ref, ref, fs.at[k], fr.at[y - 1, zz], dev(0, z, 1, x))

    steps = (8, 7)

    @pl.when(c == 0)
    def _():
        for p in range(8):
            yy, cc = p // 2, p % 2

            @pl.when(p != me)
            def _():
                got = gat.at[:, yy, z, pl.ds(cc * CAP, CAP), :]
                remote(got, got, p1s.at[0], p1r.at[p], dev(yy, z, cc, x)).wait_recv()

        for a in range(4):
            for d in (0, 1):
                ring_core0(a, 0, d).start()
        total = jnp.zeros((16, 128), F32)
        for p in range(8):

            @pl.when(p != me)
            def _():
                remote(ltile, lplane.at[p], ls.at[0], lr.at[p], dev(p // 2, z, p % 2, x)).wait_recv()

        for p in range(8):
            total = total + lplane[p].astype(F32)
        lall[z] = total.astype(BF16)
        for d in (0, 1):
            ring_core0(4, 0, d).start()
        for s in range(1, 9):
            for a in range(5):
                for d in (0, 1):
                    if s - 1 < steps[d]:
                        ring_core0(a, s - 1, d, 1).wait_recv()
                    if s < steps[d]:
                        ring_core0(a, s, d).start()

    @pl.when(c == 1)
    def _():
        got = gat.at[:, y, z, pl.ds(0, CAP), :]
        remote(got, got, p1s.at[0], p1r.at[y * 2], dev(y, z, 0, x)).wait_recv()
        for a in range(4):
            for d in (0, 1):
                ring_core1(a, 0, d).start()

        @pl.when(y != 0)
        def _():
            forward(z, 0).start()

        for s in range(1, 9):
            for a in range(4):
                for d in (0, 1):
                    if s - 1 < steps[d]:
                        ring_core1(a, s - 1, d, 1).wait_recv()
                    if s < steps[d]:
                        ring_core1(a, s, d).start()

            @pl.when(y != 0)
            def _():
                forward((z - s + 2 * NZ) % NZ, s).start()
                if s - 1 < steps[1]:
                    forward((z + s) % NZ, 8 + s).start()

        @pl.when(y == 0)
        def _():
            for yy in range(1, 4):
                for zz in range(NZ):
                    ref = gat.at[:, yy, zz]
                    remote(ref, ref, fs.at[0], fr.at[yy - 1, zz], dev(yy, z, 1, x)).wait_recv()

    def to_column(i):
        zz = (z + i) % NZ
        return remote(xc.at[:, window(zz)], xt.at[xt_rows, :], xts.at[i], xtr.at[z], dev(y, zz, c, x))

    for i in range(1, NZ):
        to_column(i).start()
    xt[xt_rows, :] = xc[:, window(z)]

    @pl.when(c == 0)
    def _():
        total = jnp.zeros((16, 128), F32)
        for zz in range(NZ):
            total = total + lall[zz].astype(F32)
        lsum[...] = total

    def to_sibling():
        return remote(lsum, lsum, dls, dlr, dev(0, z, 1, x))

    @pl.when((c == 0) & (y == 0))
    def _():
        to_sibling().start()

    @pl.when((c == 1) & (y == 0))
    def _():
        to_sibling().wait_recv()

    def all_rows(a):
        return gat[a].reshape(ROWS, HD)

    def to_slot_owner(i):
        yy, cc = plane[i - 1]
        mine = pl.ds(pl.multiple_of(yy * 32 + cc * CAP, CAP), CAP)
        return remote(
            ob.at[:, mine, :],
            outs.at[:, :, pl.ds(pl.multiple_of(head * HD, HD), HD)],
            outsem_s.at[i], outsem_r.at[head], dev(yy, z, cc, x),
        )

    def to_x(i):
        return remote(xg.at[x], xg.at[x], xgs.at[i], xgr.at[x], dev(y, z, c, (x + i) % NX))

    def to_plane(i):
        yy, cc = plane[i - 1]
        return remote(gps.at[yy], lgp.at[head], gs.at[i], gr.at[head], dev(yy, z, cc, x))

    @pl.when(is_owner)
    def _():
        sub = iota((128, 128), 0)
        lane = iota((128, 128), 1)
        before = (sub < lane).astype(BF16)
        base = jnp.zeros((128, 1), F32)
        for t in range(16):
            line = owner_ref[t : t + 1, :]
            names = (sub == line).astype(F32)
            count = dot(names.astype(BF16), before, 1, 0)
            rank = jnp.sum(names * (count + base), axis=0, keepdims=True)
            base = base + jnp.sum(names, axis=1, keepdims=True)
            slot[t : t + 1, :] = line.astype(F32) * 16.0 + rank
        slot[16:, :] = jnp.zeros((112, 128), F32)
        slot_col = jnp.transpose(slot[...])
        own_slot = ((sub // 32) * 512 + z * 32 + sub % 32).astype(F32)
        for t in range(16):
            cols = slice(t * 128, (t + 1) * 128)
            sel[:, cols] = (own_slot == slot[t : t + 1, :]).astype(BF16)
            column = jnp.broadcast_to(slot_col[:, t : t + 1], (128, 128))
            for u in range(16):
                pt[cols, u * 128 : (u + 1) * 128] = (column == (lane + u * 128).astype(F32)).astype(BF16)
            row16 = iota((16, 128), 0)
            lane16 = iota((16, 128), 1)
            value = jnp.where(row16 == 0, t * 8 + lane16 // 16, jnp.where(row16 == 1, lane16 % 16, 0))
            ownx[:, cols] = jnp.where(row16 == 2, lsum[t : t + 1, :], value.astype(F32)).astype(BF16)
            gating = jax.nn.sigmoid(lsum[t : t + 1, :])
            rows[2:3, cols] = gating
        own = dot(sel[...], ownx[...], 1, 1)
        own_j = own[:, 0:1] * 16.0 + own[:, 1:2]
        own_j_row = jnp.transpose(jnp.broadcast_to(own_j, (128, 128)))[0:1]
        own_logit_row = jnp.transpose(jnp.broadcast_to(own[:, 2:3], (128, 128)))[0:1]
        own_gate = jax.nn.sigmoid(own_logit_row)

        selw = sel[...]
        q_own = dot(selw, all_rows(Q), 1, 0).astype(BF16)
        k_own = dot(selw, all_rows(K), 1, 0).astype(BF16)
        v_own = dot(selw, all_rows(V), 1, 0).astype(BF16)
        g_own = gat[G, :, z].reshape(128, HD)

        vt[...] = jnp.transpose(all_rows(V))
        for t in range(4):
            part_rows = slice(t * 512, (t + 1) * 512)
            block = dot(pt[part_rows, :], all_rows(G), 1, 0)
            gc[part_rows, :] = block.astype(BF16)
            gct[:, part_rows] = jnp.transpose(block)

        for t in range(4):
            cols = slice(t * 512, (t + 1) * 512)
            q_block = gat[Q, t].reshape(512, HD)
            most = jnp.full((1, 512), -jnp.inf, F32)
            for u in range(t + 1):
                score = dot(gat[K, u].reshape(512, HD), q_block, 1, 1)
                if u == t:
                    score = jnp.where(iota((512, 512), 0) <= iota((512, 512), 1), score, -jnp.inf)
                st[u * 512 : (u + 1) * 512, :] = score
                most = jnp.maximum(most, jnp.max(score, axis=0, keepdims=True))
            total = jnp.zeros((1, 512), F32)
            for u in range(t + 1):
                keys = slice(u * 512, (u + 1) * 512)
                weight = jnp.exp((st[keys, :] - most) * SCALE)
                total = total + jnp.sum(weight, axis=0, keepdims=True)
                wt[keys, :] = weight.astype(BF16)
            n = (t + 1) * 512
            ctx = dot(vt[:, :n], wt[:n, :], 1, 0)
            gate_part = jnp.sum(ctx * gct[:, cols], axis=0, keepdims=True) / total
            gating = rows[2:3, cols]
            rows[0:1, cols] = most * SCALE + jnp.log(total)
            rows[1:2, cols] = gating * gate_part
            logit_grad = gate_part * gating * (1.0 - gating)
            for u in range(4):
                xg[x, t, u : u + 1, :] = logit_grad[:, u * 128 : (u + 1) * 128]
            xg[x, t, 4:8, :] = jnp.zeros((4, 128), F32)
        for i in range(1, NX):
            to_x(i).start()

        score = dot(all_rows(K), q_own, 1, 1)
        score = jnp.where(iota((ROWS, 128), 0).astype(F32) <= own_j_row, score, -jnp.inf)
        most = jnp.max(score, axis=0, keepdims=True)
        weight = jnp.exp((score - most) * SCALE)
        weight = (weight * (1.0 / jnp.sum(weight, axis=0, keepdims=True))).astype(BF16)
        ctx = dot(vt[...], weight, 1, 0)
        g_own_t = jnp.transpose(g_own.astype(F32))
        delta = jnp.sum(ctx * g_own_t, axis=0, keepdims=True) * own_gate
        ob[0] = jnp.transpose(ctx * own_gate).astype(BF16)
        prob_grad = dot(all_rows(V), g_own, 1, 1) * own_gate
        score_grad = (weight.astype(F32) * (prob_grad - delta)).astype(BF16)
        ob[1] = (dot(score_grad, all_rows(K), 0, 0) * SCALE).astype(BF16)

        score = dot(k_own, all_rows(Q), 1, 1) * SCALE
        causal = iota((128, ROWS), 1).astype(F32) >= own_j
        weight = jnp.exp(jnp.where(causal, score - rows[0:1, :], -jnp.inf)).astype(BF16).astype(F32)
        prob_grad = dot(v_own, gc[...], 1, 1) * rows[2:3, :]
        score_grad = (weight * (prob_grad - rows[1:2, :])).astype(BF16)
        ob[2] = (dot(score_grad, all_rows(Q), 1, 0) * SCALE).astype(BF16)
        ob[3] = dot((weight * rows[2:3, :]).astype(BF16), gc[...], 1, 0).astype(BF16)
        for i in range(1, 8):
            to_slot_owner(i).start()
        here = pl.ds(pl.multiple_of(y * 32 + c * CAP, CAP), CAP)
        outs[:, :, pl.ds(pl.multiple_of(head * HD, HD), HD)] = ob[:, here, :]

        for i in range(1, NX):
            xx = (x + i) % NX
            remote(xg.at[xx], xg.at[xx], xgs.at[0], xgr.at[xx], dev(y, z, c, xx)).wait_recv()
        gps[...] = xg[0] + xg[1] + xg[2] + xg[3]
        for i in range(1, 8):
            to_plane(i).start()
        lgp[head] = gps[y]

    for h in range(5):
        yy, cc = (h, 0) if h < 4 else (0, 1)

        @pl.when((yy != y) | (cc != c))
        def _():
            remote(lgp.at[h], lgp.at[h], gs.at[0], gr.at[h], dev(yy, z, cc, x)).wait_recv()

    for i in range(1, NZ):
        zz = (z + i) % NZ
        got = xt.at[pl.ds(pl.multiple_of(zz * 32 + c * CAP, CAP), CAP), :]
        remote(got, got, xts.at[0], xtr.at[zz], dev(y, zz, c, x)).wait_recv()
    logit_grad = lgp[0] + lgp[1] + lgp[2] + lgp[3] + lgp[4]
    total = jnp.zeros((8, 256), F32)
    for t in range(4):
        line = jnp.broadcast_to(logit_grad[t : t + 1, :], (8, 128))
        total = total + lax.dot_general(
            line, xt[t * 128 : (t + 1) * 128, :].astype(F32), (((1,), (0,)), ((), ())),
            precision=lax.Precision.HIGHEST, preferred_element_type=F32,
        )
    part[...] = total

    def to_part(cc):
        return remote(part, pr.at[me], prs.at[cc], prr.at[me], dev(x, z, cc, x))

    def to_fx(i):
        return remote(part, fx, fxs.at[i], fxr, dev(y, z, c, (x + i) % NX))

    for cc in range(2):

        @pl.when((y != x) | (c != cc))
        def _():
            to_part(cc).start()

    @pl.when(y == x)
    def _():
        pr[me] = part[...]
        for p in range(8):

            @pl.when(p != me)
            def _():
                remote(pr.at[p], pr.at[p], prs.at[0], prr.at[p], dev(p // 2, z, p % 2, x)).wait_recv()

        to_part(1 - c).wait_send()
        total = pr[0]
        for p in range(1, 8):
            total = total + pr[p]
        part[...] = total
        fx[...] = total
        for i in range(1, NX):
            to_fx(i).start()

    @pl.when(y != x)
    def _():
        remote(part, fx, fxs.at[0], fxr, dev(y, z, c, y)).wait_recv()

    offset = (z * 80) % 128 + c * 40
    router_ref[...] = pltpu.roll(fx[...], (256 - offset) % 256, 1)[:, :128]

    for h in range(5):
        yy, cc = (h, 0) if h < 4 else (0, 1)

        @pl.when((yy != y) | (cc != c))
        def _():
            got = outs.at[:, :, pl.ds(h * HD, HD)]
            remote(got, got, outsem_s.at[0], outsem_r.at[h], dev(yy, z, cc, x)).wait_recv()

    block_out_ref[...] = outs[0]
    gq_ref[...] = outs[1]
    gk_ref[...] = outs[2]
    gv_ref[...] = outs[3]

    for h in range(4):

        @pl.when((c != 0) | (y != h))
        def _():
            to_head(h, dev(h, z, 0, x)).wait_send()
            to_logit(h).wait_send()

    @pl.when(c == 0)
    def _():
        to_head(4, dev(y, z, 1, x)).wait_send()
        for s in range(8):
            for a in range(5):
                for d in (0, 1):
                    if s < steps[d]:
                        ring_core0(a, s, d).wait_send()

    @pl.when(c == 1)
    def _():
        for s in range(8):
            for a in range(4):
                for d in (0, 1):
                    if s < steps[d]:
                        ring_core1(a, s, d).wait_send()

        @pl.when(y != 0)
        def _():
            for k in range(16):
                forward(z, k).wait_send()

    @pl.when((c == 0) & (y == 0))
    def _():
        to_sibling().wait_send()

    for i in range(1, NZ):
        to_column(i).wait_send()

    @pl.when(is_owner)
    def _():
        for i in range(1, 8):
            to_slot_owner(i).wait_send()
            to_plane(i).wait_send()
        for i in range(1, NX):
            to_x(i).wait_send()

    @pl.when(y != x)
    def _():
        to_part(0).wait_send()
        to_part(1).wait_send()

    @pl.when(y == x)
    def _():
        for i in range(1, NX):
            to_fx(i).wait_send()


def body(stream, queries, keys, values, router_weight, chosen, owner, grad_out):
    vmem = pl.BlockSpec(memory_space=pltpu.VMEM)
    dma = pltpu.SemaphoreType.DMA
    wide = jax.ShapeDtypeStruct((CAP, 5 * HD), BF16)
    scratch = [
        pltpu.VMEM((128, 5120), BF16),
        pltpu.VMEM((4, CAP, 5 * HD), BF16),
        pltpu.VMEM((4, NY, NZ, 32, HD), BF16),
        pltpu.VMEM((CAP, 5248), BF16),
        pltpu.VMEM((512, 256), BF16),
        pltpu.VMEM((16, 128), BF16),
        pltpu.VMEM((8, 16, 128), BF16),
        pltpu.VMEM((NZ, 16, 128), BF16),
        pltpu.VMEM((16, 128), F32),
        pltpu.VMEM((128, 128), F32),
        pltpu.VMEM((ROWS, ROWS), BF16),
        pltpu.VMEM((128, ROWS), BF16),
        pltpu.VMEM((16, ROWS), BF16),
        pltpu.VMEM((ROWS, 512), F32),
        pltpu.VMEM((ROWS, 512), BF16),
        pltpu.VMEM((HD, ROWS), BF16),
        pltpu.VMEM((HD, ROWS), F32),
        pltpu.VMEM((ROWS, HD), BF16),
        pltpu.VMEM((8, ROWS), F32),
        pltpu.VMEM((4, 128, HD), BF16),
        pltpu.VMEM((4, CAP, 5 * HD), BF16),
        pltpu.VMEM((NX, NY, 8, 128), F32),
        pltpu.VMEM((NY, 8, 128), F32),
        pltpu.VMEM((5, 8, 128), F32),
        pltpu.VMEM((8, 256), F32),
        pltpu.VMEM((8, 8, 256), F32),
        pltpu.VMEM((8, 256), F32),
        dma, dma((5,)), dma((8,)), dma((4,)), dma((8,)),
        dma((2, 5, 8)), dma((2, 5, 8)), dma((16,)), dma((3, 16)), dma, dma,
        dma((16,)), dma((16,)), dma((8,)), dma((5,)),
        dma((4,)), dma((4,)), dma((8,)), dma((5,)), dma((2,)), dma((8,)), dma((4,)), dma,
    ]
    *big, router = pl.pallas_call(
        kernel,
        out_shape=(wide, wide, wide, wide, jax.ShapeDtypeStruct((8, 128), F32)),
        in_specs=[pl.BlockSpec(memory_space=pltpu.SMEM)] + [vmem] * 6 + [pl.BlockSpec(memory_space=pl.ANY)],
        out_specs=(vmem,) * 5,
        scratch_shapes=scratch,
        compiler_params=pltpu.CompilerParams(
            collective_id=0, has_side_effects=True, vmem_limit_bytes=48 * 2**20
        ),
        name="routed_attention",
    )(
        chosen, owner.reshape(16, 128), router_weight.reshape(1, -1),
        queries, keys, values, grad_out, stream,
    )
    return (*big, router[0, :40])


def solution(mesh):
    return jax.shard_map(
        body,
        mesh=mesh,
        in_specs=(
            P("seq", None),
            P("seq", "head"),
            P("seq", "head"),
            P("seq", "head"),
            P(),
            P(),
            P(),
            P("seq", "head"),
        ),
        out_specs=(
            P("seq", "head"),
            P("seq", "head"),
            P("seq", "head"),
            P("seq", "head"),
            P("seq"),
        ),
        check_vma=False,
    )
```

```python
import jax
import jax.numpy as jnp
from jax import lax
from jax.experimental import pallas as pl
from jax.experimental.pallas import tpu as pltpu
from jax.sharding import PartitionSpec as P

NY, NZ, NX = 4, 16, 4
CAP = 16
HD = 128
ROWS = 2048
SCALE = HD**-0.5
MESH = pl.DeviceIdType.MESH
Q, K, G, V = 0, 1, 2, 3
F32, BF16 = jnp.float32, jnp.bfloat16


def dot(a, b, ca, cb):
    return lax.dot_general(a, b, (((ca,), (cb,)), ((), ())), preferred_element_type=F32)


def iota(shape, dim):
    return lax.broadcasted_iota(jnp.int32, shape, dim)


def kernel(
    chosen_ref, owner_in, weight_in, q_in, k_in, v_in, g_in, stream_in,
    out_ref, router_ref,
    xs, qin, kin, vin, win, own_ref, pk, gat, ring, quarter, xc, xt, ltile, lplane, lall, lsum,
    slot, pt, sel, ownx, st, wt, wo, w2, vt, gct, gc, rows, ob, outs,
    gl, lgx, part, pr,
    sem_in, p1s, p1r, qr_s, qr_r, ls, lr, rs, rr, ffs, ffr, qfs, fr, dls, dlr, xts, xtr,
    outsem_s, outsem_r, gs, gr, prs, prr, xready,
):
    seq, x = lax.axis_index("seq"), lax.axis_index("head")
    y, z, c = seq // 32, (seq // 2) % NZ, seq % 2
    me = y * 2 + c
    is_owner = (c == 0) | (y == 0)
    head = y * (1 - c) + 4 * c
    mine = x * 5 + head

    def dev(yy, zz, cc, xx):
        return (yy * 32 + zz * 2 + cc, xx)

    def remote(src, dst, ss, rsem, target):
        return pltpu.make_async_remote_copy(
            src_ref=src, dst_ref=dst, send_sem=ss, recv_sem=rsem, device_id=target, device_id_type=MESH
        )

    def signal(sem, target):
        pl.semaphore_signal(sem, inc=1, device_id=target, device_id_type=MESH)

    loads = [
        pltpu.make_async_copy(src, dst, sem_in.at[i])
        for i, (src, dst) in enumerate(
            [
                (q_in, qin), (k_in, kin), (v_in, vin), (g_in, pk.at[G]),
                (stream_in, xs), (weight_in, win), (owner_in, own_ref),
            ]
        )
    ]
    for load in loads:
        load.start()
    xt[...] = jnp.zeros_like(xt)

    plane = []
    for i in range(1, 8):
        p = (me + i) % 8
        plane.append((p // 2, p % 2))
    peers = [dev(yy, z, cc, x) for yy, cc in plane]
    peers += [dev(y, (z + i) % NZ, c, x) for i in (1, NZ - 1)]
    peers += [dev(y, z, c, (x + i) % NX) for i in range(1, NX)]
    barrier = pltpu.get_barrier_semaphore()
    for p in peers:
        signal(barrier, p)

    token = jnp.zeros((CAP, 128), jnp.int32)
    for r in range(CAP):
        token = jnp.where(iota((CAP, 128), 0) == r, chosen_ref[seq * CAP + r] - seq * 128, token)
    pick = (token == iota((CAP, 128), 1)).astype(BF16)
    for load in loads[:4]:
        load.wait()
    pk[Q] = dot(pick, qin[...], 1, 0).astype(BF16)
    pk[K] = dot(pick, kin[...], 1, 0).astype(BF16)
    pk[V] = dot(pick, vin[...], 1, 0).astype(BF16)
    for load in loads[4:]:
        load.wait()
    for t in range(5):
        cols = slice(t * 1024, (t + 1) * 1024)
        xc[:, cols] = dot(pick, xs[:, cols], 1, 0).astype(BF16)
    xc[:, 5120:] = jnp.zeros((CAP, 128), BF16)
    logit = jnp.sum(xc[:, :5120].astype(F32) * win[...].astype(F32), axis=1, keepdims=True)
    spread = jnp.where(
        iota((CAP, 128), 1) == (seq % 8) * CAP + iota((CAP, 128), 0), logit, jnp.zeros((), F32)
    )
    line = jnp.sum(spread, axis=0, keepdims=True)
    ltile[...] = jnp.where(iota((16, 128), 0) == seq // 8, line, jnp.zeros((), F32)).astype(BF16)

    pl.semaphore_wait(barrier, len(peers))

    my_rows = pl.ds(pl.multiple_of(c * CAP, CAP), CAP)

    def to_head(h, cc):
        src = pk.at[2 * cc : 2 * cc + 2, :, pl.ds(h * HD, HD)]
        dst = gat.at[0:2, y, z, my_rows, :] if cc == 0 else ring.at[:, y, z, my_rows, :]
        return remote(src, dst, p1s.at[h, cc], p1r.at[me], dev(h, z, cc, x))

    def to_quarter(cc):
        src = pk.at[2 * cc : 2 * cc + 2, :, pl.ds(4 * HD, HD)]
        dst = quarter.at[:, z, my_rows, :] if cc == 0 else gat.at[2:4, y, z, my_rows, :]
        return remote(src, dst, qr_s, qr_r, dev(y, z, cc, x))

    def to_logit(h):
        return remote(ltile, lplane.at[me], ls.at[h], lr.at[me], dev(h, z, 0, x))

    for h in range(4):
        for cc in range(2):
            here = (c == cc) & (y == h)

            @pl.when(jnp.logical_not(here))
            def _():
                to_head(h, cc).start()

    for h in range(4):

        @pl.when((c != 0) | (y != h))
        def _():
            to_logit(h).start()

    @pl.when(c == 0)
    def _():
        to_quarter(1).start()
        gat[0:2, y, z, my_rows, :] = pk[0:2, :, pl.ds(pl.multiple_of(y * HD, HD), HD)]
        quarter[:, z, my_rows, :] = pk[0:2, :, 4 * HD : 5 * HD]
        lplane[me] = ltile[...]

    @pl.when(c == 1)
    def _():
        to_quarter(0).start()
        ring[:, y, z, my_rows, :] = pk[2:4, :, pl.ds(pl.multiple_of(y * HD, HD), HD)]
        gat[2:4, y, z, my_rows, :] = pk[2:4, :, 4 * HD : 5 * HD]

    for i in range(1, NX):
        signal(xready, dev(y, z, c, (x + i) % NX))

    def piece(cc, a, zz):
        if a == 3:
            return lall.at[zz]
        if a == 2:
            return quarter.at[:, zz] if cc == 0 else gat.at[2:4, y, zz]
        return gat.at[a, :, zz] if cc == 0 else ring.at[a, :, zz]

    def at_distance(s, d):
        return (z - s + 2 * NZ) % NZ if d == 0 else (z + s) % NZ

    def hop(cc, a, s, d, ahead=0):
        ref = piece(cc, a, at_distance(s + ahead, d))
        to = (z + 1) % NZ if d == 0 else (z + NZ - 1) % NZ
        return remote(ref, ref, rs.at[d, a, s], rr.at[d, a, s], dev(y, to, c, x))

    def to_core0(a, zz):
        return remote(ring.at[a, :, zz], gat.at[2 + a, :, zz], ffs.at[a, zz], ffr.at[a, zz], dev(y, z, 0, x))

    def to_head4(cc, zz):
        src = piece(cc, 2, zz)
        return remote(src, gat.at[2 * cc : 2 * cc + 2, y, zz], qfs.at[zz], fr.at[y * 2 + cc, zz], dev(0, z, 1, x))

    def send_quarter(cc, zz):
        if cc == 0:
            to_head4(0, zz).start()
        else:

            @pl.when(y != 0)
            def _():
                to_head4(1, zz).start()

    steps = (8, 7)

    def first_hops(cc):
        for p in range(8):
            yy, pc = p // 2, p % 2
            got = gat.at[0:2, yy, z, pl.ds(pc * CAP, CAP), :] if cc == 0 else ring.at[:, yy, z, pl.ds(pc * CAP, CAP), :]

            @pl.when(p != me)
            def _():
                remote(got, got, p1s.at[0, 0], p1r.at[p], dev(yy, z, pc, x)).wait_recv()

        for a in range(2):
            for d in (0, 1):
                hop(cc, a, 0, d).start()
        if cc == 1:
            to_core0(0, z).start()
            to_core0(1, z).start()
        sib = pl.ds((1 - cc) * CAP, CAP)
        got = quarter.at[:, z, sib, :] if cc == 0 else gat.at[2:4, y, z, sib, :]
        remote(got, got, qr_s, qr_r, dev(y, z, 1 - cc, x)).wait_recv()
        for d in (0, 1):
            hop(cc, 2, 0, d).start()
        send_quarter(cc, z)

    def next_hops(cc, pieces, s):
        for a in range(pieces):
            for d in (0, 1):
                if s - 1 < steps[d]:
                    hop(cc, a, s - 1, d, 1).wait_recv()
                if s < steps[d]:
                    hop(cc, a, s, d).start()
                if s - 1 < steps[d]:
                    if a == 2:
                        send_quarter(cc, at_distance(s, d))
                    if a < 2 and cc == 1:
                        to_core0(a, at_distance(s, d)).start()

    @pl.when(c == 0)
    def _():
        first_hops(0)
        for p in range(8):

            @pl.when(p != me)
            def _():
                remote(ltile, lplane.at[p], ls.at[0], lr.at[p], dev(p // 2, z, p % 2, x)).wait_recv()

        total = jnp.zeros((16, 128), F32)
        for p in range(8):
            total = total + lplane[p].astype(F32)
        lall[z] = total.astype(BF16)
        for d in (0, 1):
            hop(0, 3, 0, d).start()

    @pl.when(c == 1)
    def _():
        first_hops(1)

    sub = iota((128, 128), 0)
    lane = iota((128, 128), 1)

    @pl.when(is_owner)
    def _():
        before = (sub < lane).astype(BF16)
        base = jnp.zeros((128, 1), F32)
        for t in range(16):
            line = own_ref[t : t + 1, :]
            names = (sub == line).astype(F32)
            count = dot(names.astype(BF16), before, 1, 0)
            rank = jnp.sum(names * (count + base), axis=0, keepdims=True)
            base = base + jnp.sum(names, axis=1, keepdims=True)
            slot[t : t + 1, :] = line.astype(F32) * 16.0 + rank
        slot[16:, :] = jnp.zeros((112, 128), F32)

    @pl.when(c == 0)
    def _():
        next_hops(0, 4, 1)

    @pl.when(c == 1)
    def _():
        next_hops(1, 3, 1)

    @pl.when(is_owner)
    def _():
        slot_col = jnp.transpose(slot[...])
        own_slot = ((sub // 32) * 512 + z * 32 + sub % 32).astype(F32)
        for t in range(16):
            cols = slice(t * 128, (t + 1) * 128)
            sel[:, cols] = (own_slot == slot[t : t + 1, :]).astype(BF16)
            column = jnp.broadcast_to(slot_col[:, t : t + 1], (128, 128))
            for u in range(16):
                pt[cols, u * 128 : (u + 1) * 128] = (column == (lane + u * 128).astype(F32)).astype(BF16)

    @pl.when(c == 0)
    def _():
        for s in range(2, 9):
            next_hops(0, 4, s)

    @pl.when(c == 1)
    def _():
        for s in range(2, 9):
            next_hops(1, 3, s)

    def window(zz):
        return pl.ds(pl.multiple_of(x * 1280 + (zz * 80 // 128) * 128, 128), 256)

    xt_rows = pl.ds(pl.multiple_of(z * 32 + c * CAP, CAP), CAP)

    def to_column(i):
        zz = (z + i) % NZ
        return remote(xc.at[:, window(zz)], xt.at[xt_rows, :], xts.at[i], xtr.at[z], dev(y, zz, c, x))

    for i in range(1, NZ):
        to_column(i).start()
    xt[xt_rows, :] = xc[:, window(z)]

    def to_sibling():
        return remote(lsum, lsum, dls, dlr, dev(0, z, 1, x))

    @pl.when(c == 0)
    def _():
        total = jnp.zeros((16, 128), F32)
        for zz in range(NZ):
            total = total + lall[zz].astype(F32)
        lsum[...] = total

        @pl.when(y == 0)
        def _():
            to_sibling().start()

    @pl.when((c == 1) & (y == 0))
    def _():
        to_sibling().wait_recv()
        for yy in range(4):
            for zz in range(NZ):
                ref = gat.at[0:2, yy, zz]
                remote(ref, ref, qfs.at[0], fr.at[yy * 2, zz], dev(yy, z, 0, x)).wait_recv()

    def all_rows(a):
        return gat[a].reshape(ROWS, HD)

    def to_slot_owner(i):
        yy, cc = plane[i - 1]
        theirs = pl.ds(pl.multiple_of(yy * 32 + cc * CAP, CAP), CAP)
        return remote(
            ob.at[:, theirs, :],
            outs.at[:, :, pl.ds(pl.multiple_of(head * HD, HD), HD)],
            outsem_s.at[i], outsem_r.at[head], dev(yy, z, cc, x),
        )

    def to_all(i):
        p = (me + i) % 8
        return remote(
            gl.at[p // 2], lgx.at[mine], gs.at[i], gr.at[mine], dev(p // 2, z, p % 2, (x + i // 8) % NX)
        )

    @pl.when(is_owner)
    def _():
        for t in range(16):
            cols = slice(t * 128, (t + 1) * 128)
            row16 = iota((16, 128), 0)
            lane16 = iota((16, 128), 1)
            value = jnp.where(row16 == 0, t * 8 + lane16 // 16, jnp.where(row16 == 1, lane16 % 16, 0))
            ownx[:, cols] = jnp.where(row16 == 2, lsum[t : t + 1, :], value.astype(F32)).astype(BF16)
            rows[2:3, cols] = jax.nn.sigmoid(lsum[t : t + 1, :])
        own = dot(sel[...], ownx[...], 1, 1)
        own_j = own[:, 0:1] * 16.0 + own[:, 1:2]
        own_j_row = jnp.transpose(jnp.broadcast_to(own_j, (128, 128)))[0:1]
        own_logit_row = jnp.transpose(jnp.broadcast_to(own[:, 2:3], (128, 128)))[0:1]
        own_gate = jax.nn.sigmoid(own_logit_row)

        selw = sel[...]
        q_own = dot(selw, all_rows(Q), 1, 0).astype(BF16)
        k_own = dot(selw, all_rows(K), 1, 0).astype(BF16)

        for t in range(4):
            cols = slice(t * 512, (t + 1) * 512)
            q_block = gat[Q, t].reshape(512, HD)
            most = jnp.full((1, 512), -jnp.inf, F32)
            for u in range(t + 1):
                score = dot(gat[K, u].reshape(512, HD), q_block, 1, 1)
                if u == t:
                    score = jnp.where(iota((512, 512), 0) <= iota((512, 512), 1), score, -jnp.inf)
                st[u * 512 : (u + 1) * 512, :] = score
                most = jnp.maximum(most, jnp.max(score, axis=0, keepdims=True))
            total = jnp.zeros((1, 512), F32)
            for u in range(t + 1):
                keys = slice(u * 512, (u + 1) * 512)
                weight = jnp.exp((st[keys, :] - most) * SCALE)
                total = total + jnp.sum(weight, axis=0, keepdims=True)
                wt[keys, cols] = weight.astype(BF16)
            rows[0:1, cols] = most * SCALE + jnp.log(total)
            rows[3:4, cols] = 1.0 / total

        score = dot(all_rows(K), q_own, 1, 1)
        score = jnp.where(iota((ROWS, 128), 0).astype(F32) <= own_j_row, score, -jnp.inf)
        most = jnp.max(score, axis=0, keepdims=True)
        weight = jnp.exp((score - most) * SCALE)
        wo[...] = (weight * (1.0 / jnp.sum(weight, axis=0, keepdims=True))).astype(BF16)

        score = dot(k_own, all_rows(Q), 1, 1) * SCALE
        causal = iota((128, ROWS), 1).astype(F32) >= own_j
        w2[...] = jnp.exp(jnp.where(causal, score - rows[0:1, :], -jnp.inf)).astype(BF16)

        @pl.when(c == 0)
        def _():
            for zz in range(NZ):
                for a in range(2):
                    to_core0(a, zz).wait_recv()

        @pl.when(c == 1)
        def _():
            for yy in range(1, 4):
                for zz in range(NZ):
                    ref = gat.at[2:4, yy, zz]
                    remote(ref, ref, qfs.at[0], fr.at[yy * 2 + 1, zz], dev(yy, z, 1, x)).wait_recv()

        vt[...] = jnp.transpose(all_rows(V))
        for t in range(4):
            part_rows = slice(t * 512, (t + 1) * 512)
            block = dot(pt[part_rows, :], all_rows(G), 1, 0)
            gc[part_rows, :] = block.astype(BF16)
            gct[:, part_rows] = jnp.transpose(block)
        for t in range(4):
            cols = slice(t * 512, (t + 1) * 512)
            n = (t + 1) * 512
            ctx = dot(vt[:, :n], wt[:n, cols], 1, 0)
            gate_part = jnp.sum(ctx * gct[:, cols], axis=0, keepdims=True) * rows[3:4, cols]
            gating = rows[2:3, cols]
            rows[1:2, cols] = gating * gate_part
            logit_grad = gate_part * gating * (1.0 - gating)
            for u in range(4):
                gl[t, u : u + 1, :] = logit_grad[:, u * 128 : (u + 1) * 128]
            gl[t, 4:8, :] = jnp.zeros((4, 128), F32)
        pl.semaphore_wait(xready, 3)
        for i in range(1, 32):
            to_all(i).start()
        lgx[mine] = gl[y]

        v_own = dot(selw, all_rows(V), 1, 0).astype(BF16)
        g_own = gat[G, :, z].reshape(128, HD)
        ctx = dot(vt[...], wo[...], 1, 0)
        g_own_t = jnp.transpose(g_own.astype(F32))
        delta = jnp.sum(ctx * g_own_t, axis=0, keepdims=True) * own_gate
        ob[0] = jnp.transpose(ctx * own_gate).astype(BF16)
        prob_grad = dot(all_rows(V), g_own, 1, 1) * own_gate
        score_grad = (wo[...].astype(F32) * (prob_grad - delta)).astype(BF16)
        ob[1] = (dot(score_grad, all_rows(K), 0, 0) * SCALE).astype(BF16)

        weight = w2[...].astype(F32)
        prob_grad = dot(v_own, gc[...], 1, 1) * rows[2:3, :]
        score_grad = (weight * (prob_grad - rows[1:2, :])).astype(BF16)
        ob[2] = (dot(score_grad, all_rows(Q), 1, 0) * SCALE).astype(BF16)
        ob[3] = dot((weight * rows[2:3, :]).astype(BF16), gc[...], 1, 0).astype(BF16)
        for i in range(1, 8):
            to_slot_owner(i).start()
        here = pl.ds(pl.multiple_of(y * 32 + c * CAP, CAP), CAP)
        outs[:, :, pl.ds(pl.multiple_of(head * HD, HD), HD)] = ob[:, here, :]

    @pl.when(jnp.logical_not(is_owner))
    def _():
        pl.semaphore_wait(xready, 3)

    for i in range(1, NZ):
        zz = (z + i) % NZ
        got = xt.at[pl.ds(pl.multiple_of(zz * 32 + c * CAP, CAP), CAP), :]
        remote(got, got, xts.at[0], xtr.at[zz], dev(y, zz, c, x)).wait_recv()
    for p in range(20):
        xx, h = p // 5, p % 5
        yy, cc = (h, 0) if h < 4 else (0, 1)

        @pl.when((p != mine) | jnp.logical_not(is_owner))
        def _():
            remote(lgx.at[p], lgx.at[p], gs.at[0], gr.at[p], dev(yy, z, cc, xx)).wait_recv()

    logit_grad = lgx[0]
    for p in range(1, 20):
        logit_grad = logit_grad + lgx[p]
    total = jnp.zeros((8, 256), F32)
    for t in range(4):
        line = jnp.broadcast_to(logit_grad[t : t + 1, :], (8, 128))
        total = total + lax.dot_general(
            line, xt[t * 128 : (t + 1) * 128, :].astype(F32), (((1,), (0,)), ((), ())),
            precision=lax.Precision.HIGHEST, preferred_element_type=F32,
        )
    part[...] = total

    def to_part(xx, cc):
        return remote(part, pr.at[me], prs.at[xx, cc], prr.at[me], dev(x, z, cc, xx))

    def is_me(xx, cc):
        return (y == x) & (x == xx) & (c == cc)

    for xx in range(4):
        for cc in range(2):

            @pl.when(jnp.logical_not(is_me(xx, cc)))
            def _():
                to_part(xx, cc).start()

    @pl.when(y == x)
    def _():
        pr[me] = part[...]

    for p in range(8):

        @pl.when((p != me) | (y != x))
        def _():
            remote(pr.at[p], pr.at[p], prs.at[0, 0], prr.at[p], dev(p // 2, z, p % 2, y)).wait_recv()

    total = pr[0]
    for p in range(1, 8):
        total = total + pr[p]
    offset = (z * 80) % 128 + c * 40
    router_ref[...] = pltpu.roll(total, (256 - offset) % 256, 1)[:, :128]

    for h in range(5):
        yy, cc = (h, 0) if h < 4 else (0, 1)

        @pl.when((yy != y) | (cc != c))
        def _():
            got = outs.at[:, :, pl.ds(h * HD, HD)]
            remote(got, got, outsem_s.at[0], outsem_r.at[h], dev(yy, z, cc, x)).wait_recv()

    out_ref[...] = outs[...]

    for h in range(4):
        for cc in range(2):

            @pl.when((c != cc) | (y != h))
            def _():
                to_head(h, cc).wait_send()

        @pl.when((c != 0) | (y != h))
        def _():
            to_logit(h).wait_send()

    @pl.when(c == 0)
    def _():
        to_quarter(1).wait_send()
        for s in range(8):
            for a in range(4):
                for d in (0, 1):
                    if s < steps[d]:
                        hop(0, a, s, d).wait_send()
        for zz in range(NZ):
            to_head4(0, zz).wait_send()

        @pl.when(y == 0)
        def _():
            to_sibling().wait_send()

    @pl.when(c == 1)
    def _():
        to_quarter(0).wait_send()
        for s in range(8):
            for a in range(3):
                for d in (0, 1):
                    if s < steps[d]:
                        hop(1, a, s, d).wait_send()
        for zz in range(NZ):
            to_core0(0, zz).wait_send()
            to_core0(1, zz).wait_send()

        @pl.when(y != 0)
        def _():
            for zz in range(NZ):
                to_head4(1, zz).wait_send()

    for i in range(1, NZ):
        to_column(i).wait_send()

    @pl.when(is_owner)
    def _():
        for i in range(1, 8):
            to_slot_owner(i).wait_send()
        for i in range(1, 32):
            to_all(i).wait_send()

    for xx in range(4):
        for cc in range(2):

            @pl.when(jnp.logical_not(is_me(xx, cc)))
            def _():
                to_part(xx, cc).wait_send()


def body(stream, queries, keys, values, router_weight, chosen, owner, grad_out):
    vmem = pl.BlockSpec(memory_space=pltpu.VMEM)
    hbm = pl.BlockSpec(memory_space=pl.ANY)
    dma = pltpu.SemaphoreType.DMA
    scratch = [
        pltpu.VMEM((128, 5120), BF16),
        pltpu.VMEM((128, 5 * HD), BF16),
        pltpu.VMEM((128, 5 * HD), BF16),
        pltpu.VMEM((128, 5 * HD), BF16),
        pltpu.VMEM((1, 5120), BF16),
        pltpu.VMEM((16, 128), jnp.int32),
        pltpu.VMEM((4, CAP, 5 * HD), BF16),
        pltpu.VMEM((4, NY, NZ, 32, HD), BF16),
        pltpu.VMEM((2, NY, NZ, 32, HD), BF16),
        pltpu.VMEM((2, NZ, 32, HD), BF16),
        pltpu.VMEM((CAP, 5248), BF16),
        pltpu.VMEM((512, 256), BF16),
        pltpu.VMEM((16, 128), BF16),
        pltpu.VMEM((8, 16, 128), BF16),
        pltpu.VMEM((NZ, 16, 128), BF16),
        pltpu.VMEM((16, 128), F32),
        pltpu.VMEM((128, 128), F32),
        pltpu.VMEM((ROWS, ROWS), BF16),
        pltpu.VMEM((128, ROWS), BF16),
        pltpu.VMEM((16, ROWS), BF16),
        pltpu.VMEM((ROWS, 512), F32),
        pltpu.VMEM((ROWS, ROWS), BF16),
        pltpu.VMEM((ROWS, 128), BF16),
        pltpu.VMEM((128, ROWS), BF16),
        pltpu.VMEM((HD, ROWS), BF16),
        pltpu.VMEM((HD, ROWS), F32),
        pltpu.VMEM((ROWS, HD), BF16),
        pltpu.VMEM((8, ROWS), F32),
        pltpu.VMEM((4, 128, HD), BF16),
        pltpu.VMEM((4, CAP, 5 * HD), BF16),
        pltpu.VMEM((NY, 8, 128), F32),
        pltpu.VMEM((20, 8, 128), F32),
        pltpu.VMEM((8, 256), F32),
        pltpu.VMEM((8, 8, 256), F32),
        dma((7,)), dma((4, 2)), dma((8,)), dma, dma, dma((4,)), dma((8,)),
        dma((2, 4, 8)), dma((2, 4, 8)), dma((2, 16)), dma((2, 16)), dma((16,)), dma((8, 16)), dma, dma,
        dma((16,)), dma((16,)), dma((8,)), dma((5,)), dma((32,)), dma((20,)), dma((4, 2)), dma((8,)),
        pltpu.SemaphoreType.REGULAR,
    ]
    out, router = pl.pallas_call(
        kernel,
        out_shape=(
            jax.ShapeDtypeStruct((4, CAP, 5 * HD), BF16),
            jax.ShapeDtypeStruct((8, 128), F32),
        ),
        in_specs=[pl.BlockSpec(memory_space=pltpu.SMEM)] + [hbm] * 7,
        out_specs=(vmem,) * 2,
        scratch_shapes=scratch,
        compiler_params=pltpu.CompilerParams(
            collective_id=0, has_side_effects=True, vmem_limit_bytes=56 * 2**20
        ),
        name="routed_attention",
    )(
        chosen, owner.reshape(16, 128), router_weight.reshape(1, -1),
        queries, keys, values, grad_out, stream,
    )

    def split(out_ref, router_in, *refs):
        for i in range(4):
            refs[i][...] = out_ref[i]
        refs[4][...] = router_in[...]

    wide = jax.ShapeDtypeStruct((CAP, 5 * HD), BF16)
    *big, router = pl.pallas_call(
        split,
        out_shape=(wide, wide, wide, wide, jax.ShapeDtypeStruct((8, 128), F32)),
        in_specs=[vmem] * 2,
        out_specs=(vmem,) * 5,
        name="split_outputs",
    )(out, router)
    return (*big, router[0, :40])


def solution(mesh):
    return jax.shard_map(
        body,
        mesh=mesh,
        in_specs=(
            P("seq", None),
            P("seq", "head"),
            P("seq", "head"),
            P("seq", "head"),
            P(),
            P(),
            P(),
            P("seq", "head"),
        ),
        out_specs=(
            P("seq", "head"),
            P("seq", "head"),
            P("seq", "head"),
            P("seq", "head"),
            P("seq"),
        ),
        check_vma=False,
    )
```

```python
import jax
import jax.numpy as jnp
from jax import lax
from jax.experimental import pallas as pl
from jax.experimental.pallas import tpu as pltpu
from jax.sharding import PartitionSpec as P

NY, NZ, NX = 4, 16, 4
CAP = 16
HD = 128
ROWS = 2048
SCALE = HD**-0.5
MESH = pl.DeviceIdType.MESH
Q, K, G, V = 0, 1, 2, 3
F32, BF16 = jnp.float32, jnp.bfloat16


def dot(a, b, ca, cb):
    return lax.dot_general(a, b, (((ca,), (cb,)), ((), ())), preferred_element_type=F32)


def iota(shape, dim):
    return lax.broadcasted_iota(jnp.int32, shape, dim)


def kernel(
    chosen_ref, owner_in, weight_in, q_in, k_in, v_in, g_in, stream_in,
    out_ref, router_ref,
    xs, qin, kin, vin, win, own_ref, pk, gat, ring, xc, xt, ltile, lplane, lall, lsum,
    slot, pt, sel, ownx, st, wt, wo, w2, vt, gct, gc, rows, ob, outs,
    gl, lgx, part, pr,
    sem_in, p1s, p1r, qr_s, qr_r, ls, lr, rs, rr, ffs, ffr, qfs, fr, dls, dlr, xts, xtr,
    outsem_s, outsem_r, gs, gr, prs, prr, xready,
):
    seq, x = lax.axis_index("seq"), lax.axis_index("head")
    y, z, c = seq // 32, (seq // 2) % NZ, seq % 2
    me = y * 2 + c
    is_owner = (c == 0) | (y == 0)
    head = y * (1 - c) + 4 * c
    mine = x * 5 + head

    def dev(yy, zz, cc, xx):
        return (yy * 32 + zz * 2 + cc, xx)

    def remote(src, dst, ss, rsem, target):
        return pltpu.make_async_remote_copy(
            src_ref=src, dst_ref=dst, send_sem=ss, recv_sem=rsem, device_id=target, device_id_type=MESH
        )

    def signal(sem, target):
        pl.semaphore_signal(sem, inc=1, device_id=target, device_id_type=MESH)

    loads = [
        pltpu.make_async_copy(src, dst, sem_in.at[i])
        for i, (src, dst) in enumerate(
            [
                (q_in, qin), (k_in, kin), (v_in, vin), (g_in, pk.at[G]),
                (stream_in, xs), (weight_in, win), (owner_in, own_ref),
            ]
        )
    ]
    for load in loads:
        load.start()
    xt[...] = jnp.zeros_like(xt)

    plane = []
    for i in range(1, 8):
        p = (me + i) % 8
        plane.append((p // 2, p % 2))
    peers = [dev(yy, z, cc, x) for yy, cc in plane]
    peers += [dev(y, (z + i) % NZ, c, x) for i in (1, NZ - 1, 4, NZ - 4)]
    peers += [dev(y, z, c, (x + i) % NX) for i in range(1, NX)]
    barrier = pltpu.get_barrier_semaphore()
    for p in peers:
        signal(barrier, p)

    token = jnp.zeros((CAP, 128), jnp.int32)
    for r in range(CAP):
        token = jnp.where(iota((CAP, 128), 0) == r, chosen_ref[seq * CAP + r] - seq * 128, token)
    pick = (token == iota((CAP, 128), 1)).astype(BF16)
    for load in loads[:4]:
        load.wait()
    pk[Q] = dot(pick, qin[...], 1, 0).astype(BF16)
    pk[K] = dot(pick, kin[...], 1, 0).astype(BF16)
    pk[V] = dot(pick, vin[...], 1, 0).astype(BF16)
    pl.semaphore_wait(barrier, len(peers))

    my_rows = pl.ds(pl.multiple_of(c * CAP, CAP), CAP)

    def to_head(h, cc):
        src = pk.at[2 - 2 * cc : 4 - 2 * cc, :, pl.ds(h * HD, HD)]
        dst = gat.at[2:4, y, z, my_rows, :] if cc == 0 else ring.at[:, y, z, my_rows, :]
        return remote(src, dst, p1s.at[h, cc], p1r.at[me], dev(h, z, cc, x))

    def to_quarter():
        src = pk.at[:, :, pl.ds(4 * HD, HD)]
        return remote(src, gat.at[:, y, z, my_rows, :], qr_s, qr_r, dev(y, z, 1, x))

    def to_logit(h):
        return remote(ltile, lplane.at[me], ls.at[h], lr.at[me], dev(h, z, 0, x))

    for h in range(4):
        for cc in range(2):
            here = (c == cc) & (y == h)

            @pl.when(jnp.logical_not(here))
            def _():
                to_head(h, cc).start()

    @pl.when(c == 0)
    def _():
        to_quarter().start()
        gat[2:4, y, z, my_rows, :] = pk[2:4, :, pl.ds(pl.multiple_of(y * HD, HD), HD)]

    @pl.when(c == 1)
    def _():
        ring[:, y, z, my_rows, :] = pk[0:2, :, pl.ds(pl.multiple_of(y * HD, HD), HD)]
        gat[:, y, z, my_rows, :] = pk[:, :, 4 * HD : 5 * HD]

    for load in loads[4:]:
        load.wait()
    for t in range(5):
        cols = slice(t * 1024, (t + 1) * 1024)
        xc[:, cols] = dot(pick, xs[:, cols], 1, 0).astype(BF16)
    xc[:, 5120:] = jnp.zeros((CAP, 128), BF16)
    logit = jnp.sum(xc[:, :5120].astype(F32) * win[...].reshape(1, 5120).astype(F32), axis=1, keepdims=True)
    spread = jnp.where(
        iota((CAP, 128), 1) == (seq % 8) * CAP + iota((CAP, 128), 0), logit, jnp.zeros((), F32)
    )
    line = jnp.sum(spread, axis=0, keepdims=True)
    ltile[...] = jnp.where(iota((16, 128), 0) == seq // 8, line, jnp.zeros((), F32)).astype(BF16)

    for h in range(4):

        @pl.when((c != 0) | (y != h))
        def _():
            to_logit(h).start()

    @pl.when(c == 0)
    def _():
        lplane[me] = ltile[...]

    for i in range(1, NX):
        signal(xready, dev(y, z, c, (x + i) % NX))

    paths = (
        (((0, 1), (0, 4)), ((1, 2), (4, 5)), ((2, 3), (5, 6)), ((6, 7),), ((7, 8),)),
        (((0, 1),), ((1, 2),), ((2, 3),), ((3, 4),), ((4, 5),), ((5, 6),), ((6, 7),), ((7, 8),)),
    )
    most_far = (8, 7)
    pieces = (3, 4)

    def piece(cc, a, zz):
        if cc == 0:
            return lall.at[zz] if a == 2 else gat.at[2 + a, :, zz]
        return gat.at[0:2, y, zz] if a == 0 else gat.at[2:4, y, zz] if a == 3 else ring.at[a - 1, :, zz]

    def at_distance(s, d):
        return (z - s + 2 * NZ) % NZ if d == 0 else (z + s) % NZ

    def hop(cc, a, near, far, d):
        ref = piece(cc, a, at_distance(near, d))
        to = (z + far - near) % NZ if d == 0 else (z + near - far + NZ) % NZ
        return remote(ref, ref, rs.at[d, a, far], rr.at[d, a, far], dev(y, to, c, x))

    def arrival(cc, a, far, d):
        ref = piece(cc, a, at_distance(far, d))
        return remote(ref, ref, rs.at[d, a, far], rr.at[d, a, far], dev(y, z, c, x))

    def to_core0(a, zz):
        return remote(ring.at[a, :, zz], gat.at[a, :, zz], ffs.at[a, zz], ffr.at[a, zz], dev(y, z, 0, x))

    def to_head4(b, zz):
        ref = gat.at[2 * b : 2 * b + 2, y, zz]
        return remote(ref, ref, qfs.at[b, zz], fr.at[b, y, zz], dev(0, z, 1, x))

    def pass_on(a, zz):
        if a in (0, 3):

            @pl.when(y != 0)
            def _():
                to_head4(a // 3, zz).start()
        else:
            to_core0(a - 1, zz).start()

    def hops(cc, a, level):
        for near, far in paths[cc][level]:
            for d in (0, 1):
                if near > 0:
                    arrival(cc, a, near, d).wait_recv()
                if far <= most_far[d]:
                    hop(cc, a, near, far, d).start()
                if cc == 1:
                    pass_on(a, at_distance(near, d)) if near > 0 or (d == 0 and far == 1) else None

    def all_hops(cc, levels):
        for level in levels:
            for a in range(pieces[cc]):
                hops(cc, a, level)

    def last_arrivals(cc):
        starts = [near for level in paths[cc] for near, _ in level]
        for a in range(pieces[cc]):
            for far in range(1, 9):
                for d in (0, 1):
                    if far not in starts and far <= most_far[d]:
                        arrival(cc, a, far, d).wait_recv()
                        if cc == 1:
                            pass_on(a, at_distance(far, d))

    def first_hops(cc):
        for p in range(8):
            yy, pc = p // 2, p % 2
            got = gat.at[2:4, yy, z, pl.ds(pc * CAP, CAP), :] if cc == 0 else ring.at[:, yy, z, pl.ds(pc * CAP, CAP), :]

            @pl.when(p != me)
            def _():
                remote(got, got, p1s.at[0, 0], p1r.at[p], dev(yy, z, pc, x)).wait_recv()

        if cc == 1:
            got = gat.at[:, y, z, pl.ds(0, CAP), :]
            remote(got, got, qr_s, qr_r, dev(y, z, 0, x)).wait_recv()
            all_hops(1, (0,))
        else:
            hops(0, 0, 0)
            hops(0, 1, 0)

    @pl.when(c == 0)
    def _():
        first_hops(0)
        for p in range(8):

            @pl.when(p != me)
            def _():
                remote(ltile, lplane.at[p], ls.at[0], lr.at[p], dev(p // 2, z, p % 2, x)).wait_recv()

        total = jnp.zeros((16, 128), F32)
        for p in range(8):
            total = total + lplane[p].astype(F32)
        lall[z] = total.astype(BF16)
        hops(0, 2, 0)

    @pl.when(c == 1)
    def _():
        first_hops(1)

    sub = iota((128, 128), 0)
    lane = iota((128, 128), 1)

    @pl.when(is_owner)
    def _():
        before = (sub < lane).astype(BF16)
        base = jnp.zeros((128, 1), F32)
        for t in range(16):
            line = own_ref[t : t + 1, :]
            names = (sub == line).astype(F32)
            count = dot(names.astype(BF16), before, 1, 0)
            rank = jnp.sum(names * (count + base), axis=0, keepdims=True)
            base = base + jnp.sum(names, axis=1, keepdims=True)
            slot[t : t + 1, :] = line.astype(F32) * 16.0 + rank
        slot[16:, :] = jnp.zeros((112, 128), F32)

    @pl.when(c == 0)
    def _():
        all_hops(0, (1,))

    @pl.when(c == 1)
    def _():
        all_hops(1, (1,))

    @pl.when(is_owner)
    def _():
        slot_col = jnp.transpose(slot[...])
        own_slot = ((sub // 32) * 512 + z * 32 + sub % 32).astype(F32)
        for t in range(16):
            cols = slice(t * 128, (t + 1) * 128)
            sel[:, cols] = (own_slot == slot[t : t + 1, :]).astype(BF16)
            column = jnp.broadcast_to(slot_col[:, t : t + 1], (128, 128))
            for u in range(16):
                pt[cols, u * 128 : (u + 1) * 128] = (column == (lane + u * 128).astype(F32)).astype(BF16)

    @pl.when(c == 0)
    def _():
        all_hops(0, range(2, len(paths[0])))

    @pl.when(c == 1)
    def _():
        all_hops(1, range(2, len(paths[1])))
        last_arrivals(1)

    def window(zz):
        return pl.ds(pl.multiple_of(x * 1280 + (zz * 80 // 128) * 128, 128), 256)

    xt_rows = pl.ds(pl.multiple_of(z * 32 + c * CAP, CAP), CAP)

    def to_column(i):
        zz = (z + i) % NZ
        return remote(xc.at[:, window(zz)], xt.at[xt_rows, :], xts.at[i], xtr.at[z], dev(y, zz, c, x))

    late = (3, 8, 13)

    @pl.when(c == 0)
    def _():
        for i in range(1, NZ):
            if i not in late:
                to_column(i).start()

    @pl.when(c == 1)
    def _():
        for i in range(1, NZ):
            to_column(i).start()

    xt[xt_rows, :] = xc[:, window(z)]

    def to_sibling():
        return remote(lsum, lsum, dls, dlr, dev(0, z, 1, x))

    def all_rows(a):
        return gat[a].reshape(ROWS, HD)

    def to_slot_owner(i):
        yy, cc = plane[i - 1]
        theirs = pl.ds(pl.multiple_of(yy * 32 + cc * CAP, CAP), CAP)
        return remote(
            ob.at[:, theirs, :],
            outs.at[:, :, pl.ds(pl.multiple_of(head * HD, HD), HD)],
            outsem_s.at[i], outsem_r.at[head], dev(yy, z, cc, x),
        )

    def to_all(i):
        p = (me + i) % 8
        return remote(
            gl.at[p // 2], lgx.at[mine], gs.at[i], gr.at[mine], dev(p // 2, z, p % 2, (x + i // 8) % NX)
        )

    @pl.when(is_owner)
    def _():
        @pl.when(c == 0)
        def _():
            for zz in range(NZ):
                for a in range(2):
                    to_core0(a, zz).wait_recv()

        @pl.when(c == 1)
        def _():
            for yy in range(1, 4):
                for zz in range(NZ):
                    ref = gat.at[0:2, yy, zz]
                    remote(ref, ref, qfs.at[0, 0], fr.at[0, yy, zz], dev(yy, z, 1, x)).wait_recv()

        for t in range(16):
            cols = slice(t * 128, (t + 1) * 128)
            row16 = iota((16, 128), 0)
            lane16 = iota((16, 128), 1)
            value = jnp.where(row16 == 0, t * 8 + lane16 // 16, jnp.where(row16 == 1, lane16 % 16, 0))
            ownx[:, cols] = value.astype(F32).astype(BF16)
        own = dot(sel[...], ownx[...], 1, 1)
        own_j = own[:, 0:1] * 16.0 + own[:, 1:2]
        own_j_row = jnp.transpose(jnp.broadcast_to(own_j, (128, 128)))[0:1]

        selw = sel[...]
        q_own = dot(selw, all_rows(Q), 1, 0).astype(BF16)
        k_own = dot(selw, all_rows(K), 1, 0).astype(BF16)

        for t in range(4):
            cols = slice(t * 512, (t + 1) * 512)
            q_block = gat[Q, t].reshape(512, HD)
            most = jnp.full((1, 512), -jnp.inf, F32)
            for u in range(t + 1):
                score = dot(gat[K, u].reshape(512, HD), q_block, 1, 1)
                if u == t:
                    score = jnp.where(iota((512, 512), 0) <= iota((512, 512), 1), score, -jnp.inf)
                st[u * 512 : (u + 1) * 512, :] = score
                most = jnp.maximum(most, jnp.max(score, axis=0, keepdims=True))
            total = jnp.zeros((1, 512), F32)
            for u in range(t + 1):
                keys = slice(u * 512, (u + 1) * 512)
                weight = jnp.exp((st[keys, :] - most) * SCALE)
                total = total + jnp.sum(weight, axis=0, keepdims=True)
                wt[keys, cols] = weight.astype(BF16)
            rows[0:1, cols] = most * SCALE + jnp.log(total)
            rows[3:4, cols] = 1.0 / total

        score = dot(all_rows(K), q_own, 1, 1)
        score = jnp.where(iota((ROWS, 128), 0).astype(F32) <= own_j_row, score, -jnp.inf)
        most = jnp.max(score, axis=0, keepdims=True)
        weight = jnp.exp((score - most) * SCALE)
        wo[...] = (weight * (1.0 / jnp.sum(weight, axis=0, keepdims=True))).astype(BF16)

        score = dot(k_own, all_rows(Q), 1, 1) * SCALE
        causal = iota((128, ROWS), 1).astype(F32) >= own_j
        w2[...] = jnp.exp(jnp.where(causal, score - rows[0:1, :], -jnp.inf)).astype(BF16)

        @pl.when(c == 0)
        def _():
            last_arrivals(0)
            for i in late:
                to_column(i).start()
            total = jnp.zeros((16, 128), F32)
            for zz in range(NZ):
                total = total + lall[zz].astype(F32)
            lsum[...] = total

            @pl.when(y == 0)
            def _():
                to_sibling().start()

        @pl.when(c == 1)
        def _():
            to_sibling().wait_recv()
            for yy in range(1, 4):
                for zz in range(NZ):
                    ref = gat.at[2:4, yy, zz]
                    remote(ref, ref, qfs.at[0, 0], fr.at[1, yy, zz], dev(yy, z, 1, x)).wait_recv()

        for t in range(16):
            cols = slice(t * 128, (t + 1) * 128)
            ownx[:, cols] = jnp.broadcast_to(lsum[t : t + 1, :], (16, 128)).astype(BF16)
            rows[2:3, cols] = jax.nn.sigmoid(lsum[t : t + 1, :])

        vt[...] = jnp.transpose(all_rows(V))
        for t in range(4):
            part_rows = slice(t * 512, (t + 1) * 512)
            block = dot(pt[part_rows, :], all_rows(G), 1, 0)
            gc[part_rows, :] = block.astype(BF16)
            gct[:, part_rows] = jnp.transpose(block)
        for t in range(4):
            cols = slice(t * 512, (t + 1) * 512)
            n = (t + 1) * 512
            ctx = dot(vt[:, :n], wt[:n, cols], 1, 0)
            gate_part = jnp.sum(ctx * gct[:, cols], axis=0, keepdims=True) * rows[3:4, cols]
            gating = rows[2:3, cols]
            rows[1:2, cols] = gating * gate_part
            logit_grad = gate_part * gating * (1.0 - gating)
            for u in range(4):
                gl[t, u : u + 1, :] = logit_grad[:, u * 128 : (u + 1) * 128]
            gl[t, 4:8, :] = jnp.zeros((4, 128), F32)
        pl.semaphore_wait(xready, 3)
        for i in range(1, 32):
            to_all(i).start()
        lgx[mine] = gl[y]

        own = dot(sel[...], ownx[...], 1, 1)
        own_gate = jax.nn.sigmoid(jnp.transpose(jnp.broadcast_to(own[:, 0:1], (128, 128)))[0:1])
        v_own = dot(selw, all_rows(V), 1, 0).astype(BF16)
        g_own = gat[G, :, z].reshape(128, HD)
        ctx = dot(vt[...], wo[...], 1, 0)
        g_own_t = jnp.transpose(g_own.astype(F32))
        delta = jnp.sum(ctx * g_own_t, axis=0, keepdims=True) * own_gate
        ob[0] = jnp.transpose(ctx * own_gate).astype(BF16)
        prob_grad = dot(all_rows(V), g_own, 1, 1) * own_gate
        score_grad = (wo[...].astype(F32) * (prob_grad - delta)).astype(BF16)
        ob[1] = (dot(score_grad, all_rows(K), 0, 0) * SCALE).astype(BF16)

        weight = w2[...].astype(F32)
        prob_grad = dot(v_own, gc[...], 1, 1) * rows[2:3, :]
        score_grad = (weight * (prob_grad - rows[1:2, :])).astype(BF16)
        ob[2] = (dot(score_grad, all_rows(Q), 1, 0) * SCALE).astype(BF16)
        ob[3] = dot((weight * rows[2:3, :]).astype(BF16), gc[...], 1, 0).astype(BF16)
        for i in range(1, 8):
            to_slot_owner(i).start()
        here = pl.ds(pl.multiple_of(y * 32 + c * CAP, CAP), CAP)
        outs[:, :, pl.ds(pl.multiple_of(head * HD, HD), HD)] = ob[:, here, :]

    @pl.when(jnp.logical_not(is_owner))
    def _():
        pl.semaphore_wait(xready, 3)

    for i in range(1, NZ):
        zz = (z + i) % NZ
        got = xt.at[pl.ds(pl.multiple_of(zz * 32 + c * CAP, CAP), CAP), :]
        remote(got, got, xts.at[0], xtr.at[zz], dev(y, zz, c, x)).wait_recv()
    for p in range(20):
        xx, h = p // 5, p % 5
        yy, cc = (h, 0) if h < 4 else (0, 1)

        @pl.when((p != mine) | jnp.logical_not(is_owner))
        def _():
            remote(lgx.at[p], lgx.at[p], gs.at[0], gr.at[p], dev(yy, z, cc, xx)).wait_recv()

    logit_grad = lgx[0]
    for p in range(1, 20):
        logit_grad = logit_grad + lgx[p]
    total = jnp.zeros((8, 256), F32)
    for t in range(4):
        line = jnp.broadcast_to(logit_grad[t : t + 1, :], (8, 128))
        total = total + lax.dot_general(
            line, xt[t * 128 : (t + 1) * 128, :].astype(F32), (((1,), (0,)), ((), ())),
            precision=lax.Precision.HIGHEST, preferred_element_type=F32,
        )
    part[...] = total

    def to_part(xx, cc):
        return remote(part, pr.at[me], prs.at[xx, cc], prr.at[me], dev(x, z, cc, xx))

    def is_me(xx, cc):
        return (y == x) & (x == xx) & (c == cc)

    for xx in range(4):
        for cc in range(2):

            @pl.when(jnp.logical_not(is_me(xx, cc)))
            def _():
                to_part(xx, cc).start()

    @pl.when(y == x)
    def _():
        pr[me] = part[...]

    for p in range(8):

        @pl.when((p != me) | (y != x))
        def _():
            remote(pr.at[p], pr.at[p], prs.at[0, 0], prr.at[p], dev(p // 2, z, p % 2, y)).wait_recv()

    total = pr[0]
    for p in range(1, 8):
        total = total + pr[p]
    offset = (z * 80) % 128 + c * 40
    router_ref[...] = pltpu.roll(total, (256 - offset) % 256, 1)[:, :128]

    for h in range(5):
        yy, cc = (h, 0) if h < 4 else (0, 1)

        @pl.when((yy != y) | (cc != c))
        def _():
            got = outs.at[:, :, pl.ds(h * HD, HD)]
            remote(got, got, outsem_s.at[0], outsem_r.at[h], dev(yy, z, cc, x)).wait_recv()

    out_ref[...] = outs[...]

    for h in range(4):
        for cc in range(2):

            @pl.when((c != cc) | (y != h))
            def _():
                to_head(h, cc).wait_send()

        @pl.when((c != 0) | (y != h))
        def _():
            to_logit(h).wait_send()

    def sent(cc):
        for a in range(pieces[cc]):
            for level in paths[cc]:
                for near, far in level:
                    for d in (0, 1):
                        if far <= most_far[d]:
                            hop(cc, a, near, far, d).wait_send()

    @pl.when(c == 0)
    def _():
        to_quarter().wait_send()
        sent(0)

        @pl.when(y == 0)
        def _():
            to_sibling().wait_send()

    @pl.when(c == 1)
    def _():
        sent(1)
        for zz in range(NZ):
            to_core0(0, zz).wait_send()
            to_core0(1, zz).wait_send()

        @pl.when(y != 0)
        def _():
            for zz in range(NZ):
                to_head4(0, zz).wait_send()
                to_head4(1, zz).wait_send()

    for i in range(1, NZ):
        to_column(i).wait_send()

    @pl.when(is_owner)
    def _():
        for i in range(1, 8):
            to_slot_owner(i).wait_send()
        for i in range(1, 32):
            to_all(i).wait_send()

    for xx in range(4):
        for cc in range(2):

            @pl.when(jnp.logical_not(is_me(xx, cc)))
            def _():
                to_part(xx, cc).wait_send()


def body(stream, queries, keys, values, router_weight, chosen, owner, grad_out):
    vmem = pl.BlockSpec(memory_space=pltpu.VMEM)
    hbm = pl.BlockSpec(memory_space=pl.ANY)
    dma = pltpu.SemaphoreType.DMA
    scratch = [
        pltpu.VMEM((128, 5120), BF16),
        pltpu.VMEM((128, 5 * HD), BF16),
        pltpu.VMEM((128, 5 * HD), BF16),
        pltpu.VMEM((128, 5 * HD), BF16),
        pltpu.VMEM((5120,), BF16),
        pltpu.VMEM((16, 128), jnp.int32),
        pltpu.VMEM((4, CAP, 5 * HD), BF16),
        pltpu.VMEM((4, NY, NZ, 32, HD), BF16),
        pltpu.VMEM((2, NY, NZ, 32, HD), BF16),
        pltpu.VMEM((CAP, 5248), BF16),
        pltpu.VMEM((512, 256), BF16),
        pltpu.VMEM((16, 128), BF16),
        pltpu.VMEM((8, 16, 128), BF16),
        pltpu.VMEM((NZ, 16, 128), BF16),
        pltpu.VMEM((16, 128), F32),
        pltpu.VMEM((128, 128), F32),
        pltpu.VMEM((ROWS, ROWS), BF16),
        pltpu.VMEM((128, ROWS), BF16),
        pltpu.VMEM((16, ROWS), BF16),
        pltpu.VMEM((ROWS, 512), F32),
        pltpu.VMEM((ROWS, ROWS), BF16),
        pltpu.VMEM((ROWS, 128), BF16),
        pltpu.VMEM((128, ROWS), BF16),
        pltpu.VMEM((HD, ROWS), BF16),
        pltpu.VMEM((HD, ROWS), F32),
        pltpu.VMEM((ROWS, HD), BF16),
        pltpu.VMEM((8, ROWS), F32),
        pltpu.VMEM((4, 128, HD), BF16),
        pltpu.VMEM((4, CAP, 5 * HD), BF16),
        pltpu.VMEM((NY, 8, 128), F32),
        pltpu.VMEM((20, 8, 128), F32),
        pltpu.VMEM((8, 256), F32),
        pltpu.VMEM((8, 8, 256), F32),
        dma((7,)), dma((4, 2)), dma((8,)), dma, dma, dma((4,)), dma((8,)),
        dma((2, 4, 9)), dma((2, 4, 9)), dma((2, 16)), dma((2, 16)), dma((2, 16)), dma((2, 4, 16)), dma, dma,
        dma((16,)), dma((16,)), dma((8,)), dma((5,)), dma((32,)), dma((20,)), dma((4, 2)), dma((8,)),
        pltpu.SemaphoreType.REGULAR,
    ]
    out, router = pl.pallas_call(
        kernel,
        out_shape=(
            jax.ShapeDtypeStruct((4, CAP, 5 * HD), BF16),
            jax.ShapeDtypeStruct((8, 128), F32),
        ),
        in_specs=[pl.BlockSpec(memory_space=pltpu.SMEM)] + [hbm] * 7,
        out_specs=(vmem,) * 2,
        scratch_shapes=scratch,
        compiler_params=pltpu.CompilerParams(
            collective_id=0, has_side_effects=True, vmem_limit_bytes=56 * 2**20
        ),
        name="routed_attention",
    )(
        chosen, owner.reshape(16, 128), router_weight,
        queries, keys, values, grad_out, stream,
    )

    def split(out_ref, router_in, *refs):
        for i in range(4):
            refs[i][...] = out_ref[i]
        refs[4][...] = router_in[0, :40]

    wide = jax.ShapeDtypeStruct((CAP, 5 * HD), BF16)
    return pl.pallas_call(
        split,
        out_shape=(wide, wide, wide, wide, jax.ShapeDtypeStruct((40,), F32)),
        in_specs=[vmem] * 2,
        out_specs=(vmem,) * 5,
        name="split_outputs",
    )(out, router)


def solution(mesh):
    return jax.shard_map(
        body,
        mesh=mesh,
        in_specs=(
            P("seq", None),
            P("seq", "head"),
            P("seq", "head"),
            P("seq", "head"),
            P(),
            P(),
            P(),
            P("seq", "head"),
        ),
        out_specs=(
            P("seq", "head"),
            P("seq", "head"),
            P("seq", "head"),
            P("seq", "head"),
            P("seq"),
        ),
        check_vma=False,
    )
```

```python
import jax
import jax.numpy as jnp
from jax import lax
from jax.experimental import pallas as pl
from jax.experimental.pallas import tpu as pltpu
from jax.sharding import PartitionSpec as P

NY, NZ, NX = 4, 16, 4
CAP = 16
HD = 128
ROWS = 2048
SCALE = HD**-0.5
SCALE2 = SCALE * 1.4426950408889634
MESH = pl.DeviceIdType.MESH
Q, K, G, V = 0, 1, 2, 3
F32, BF16 = jnp.float32, jnp.bfloat16


def dot(a, b, ca, cb):
    return lax.dot_general(a, b, (((ca,), (cb,)), ((), ())), preferred_element_type=F32)


def iota(shape, dim):
    return lax.broadcasted_iota(jnp.int32, shape, dim)


def kernel(
    chosen_ref, owner_in, weight_in, q_in, k_in, v_in, g_in, stream_in,
    out_ref, router_ref,
    xs, qin, kin, vin, win, own_ref, pk, gat, ring, xc, xt, ltile, lplane, lall, lsum,
    slot, pt, sel, ownx, st, wt, wo, w2, vt, gct, gc, rows, ob, outs,
    gl, lgx, part, pr,
    sem_in, p1s, p1r, qr_s, qr_r, ls, lr, rs, rr, ffs, ffr, qfs, fr, dls, dlr, xts, xtr,
    outsem_s, outsem_r, gs, gr, prs, prr, xready,
):
    seq, x = lax.axis_index("seq"), lax.axis_index("head")
    y, z, c = seq // 32, (seq // 2) % NZ, seq % 2
    me = y * 2 + c
    is_owner = (c == 0) | (y == 0)
    head = y * (1 - c) + 4 * c
    mine = x * 5 + head

    def dev(yy, zz, cc, xx):
        return (yy * 32 + zz * 2 + cc, xx)

    def remote(src, dst, ss, rsem, target):
        return pltpu.make_async_remote_copy(
            src_ref=src, dst_ref=dst, send_sem=ss, recv_sem=rsem, device_id=target, device_id_type=MESH
        )

    def signal(sem, target):
        pl.semaphore_signal(sem, inc=1, device_id=target, device_id_type=MESH)

    loads = [
        pltpu.make_async_copy(src, dst, sem_in.at[i])
        for i, (src, dst) in enumerate(
            [
                (q_in, qin), (k_in, kin), (v_in, vin), (g_in, pk.at[G]),
                (stream_in, xs), (weight_in, win), (owner_in, own_ref),
            ]
        )
    ]
    for load in loads[:4]:
        load.start()

    plane = []
    for i in range(1, 8):
        p = (me + i) % 8
        plane.append((p // 2, p % 2))
    peers = [dev(yy, z, cc, x) for yy, cc in plane]
    peers += [dev(y, (z + i) % NZ, c, x) for i in (1, NZ - 1, 4, NZ - 4)]
    peers += [dev(y, z, c, (x + i) % NX) for i in range(1, NX)]
    barrier = pltpu.get_barrier_semaphore()
    for p in peers:
        signal(barrier, p)
    for load in loads[4:]:
        load.start()

    token = jnp.zeros((CAP, 128), jnp.int32)
    for r in range(CAP):
        token = jnp.where(iota((CAP, 128), 0) == r, chosen_ref[seq * CAP + r] - seq * 128, token)
    pick = (token == iota((CAP, 128), 1)).astype(BF16)
    for load in loads[:4]:
        load.wait()
    pk[Q] = dot(pick, qin[...], 1, 0).astype(BF16)
    pk[K] = dot(pick, kin[...], 1, 0).astype(BF16)
    pk[V] = dot(pick, vin[...], 1, 0).astype(BF16)
    pl.semaphore_wait(barrier, len(peers))

    my_rows = pl.ds(pl.multiple_of(c * CAP, CAP), CAP)

    def to_head(h, cc):
        src = pk.at[2 - 2 * cc : 4 - 2 * cc, :, pl.ds(h * HD, HD)]
        dst = gat.at[2:4, y, z, my_rows, :] if cc == 0 else ring.at[:, y, z, my_rows, :]
        return remote(src, dst, p1s.at[h, cc], p1r.at[me], dev(h, z, cc, x))

    def to_quarter():
        src = pk.at[:, :, pl.ds(4 * HD, HD)]
        return remote(src, gat.at[:, y, z, my_rows, :], qr_s, qr_r, dev(y, z, 1, x))

    def to_logit(h):
        return remote(ltile, lplane.at[me], ls.at[h], lr.at[me], dev(h, z, 0, x))

    for h in range(4):
        for cc in range(2):
            here = (c == cc) & (y == h)

            @pl.when(jnp.logical_not(here))
            def _():
                to_head(h, cc).start()

    @pl.when(c == 0)
    def _():
        to_quarter().start()
        gat[2:4, y, z, my_rows, :] = pk[2:4, :, pl.ds(pl.multiple_of(y * HD, HD), HD)]

    @pl.when(c == 1)
    def _():
        ring[:, y, z, my_rows, :] = pk[0:2, :, pl.ds(pl.multiple_of(y * HD, HD), HD)]
        gat[:, y, z, my_rows, :] = pk[:, :, 4 * HD : 5 * HD]

    for load in loads[4:]:
        load.wait()
    for t in range(5):
        cols = slice(t * 1024, (t + 1) * 1024)
        xc[:, cols] = dot(pick, xs[:, cols], 1, 0).astype(BF16)
    xc[:, 5120:] = jnp.zeros((CAP, 128), BF16)
    logit = jnp.sum(xc[:, :5120].astype(F32) * win[...].reshape(1, 5120).astype(F32), axis=1, keepdims=True)
    spread = jnp.where(
        iota((CAP, 128), 1) == (seq % 8) * CAP + iota((CAP, 128), 0), logit, jnp.zeros((), F32)
    )
    line = jnp.sum(spread, axis=0, keepdims=True)
    ltile[...] = jnp.where(iota((16, 128), 0) == seq // 8, line, jnp.zeros((), F32)).astype(BF16)

    for h in range(4):

        @pl.when((c != 0) | (y != h))
        def _():
            to_logit(h).start()

    @pl.when(c == 0)
    def _():
        lplane[me] = ltile[...]

    for i in range(1, NX):
        signal(xready, dev(y, z, c, (x + i) % NX))

    paths = (
        (((0, 1), (0, 4)), ((1, 2), (4, 5)), ((2, 3), (5, 6)), ((6, 7),), ((7, 8),)),
        (((0, 1),), ((1, 2),), ((2, 3),), ((3, 4),), ((4, 5),), ((5, 6),), ((6, 7),), ((7, 8),)),
    )
    most_far = (8, 7)
    pieces = (3, 4)

    def piece(cc, a, zz):
        if cc == 0:
            return lall.at[zz] if a == 2 else gat.at[2 + a, :, zz]
        return gat.at[0:2, y, zz] if a == 0 else gat.at[2:4, y, zz] if a == 3 else ring.at[a - 1, :, zz]

    def at_distance(s, d):
        return (z - s + 2 * NZ) % NZ if d == 0 else (z + s) % NZ

    def hop(cc, a, near, far, d):
        ref = piece(cc, a, at_distance(near, d))
        to = (z + far - near) % NZ if d == 0 else (z + near - far + NZ) % NZ
        return remote(ref, ref, rs.at[d, a, far], rr.at[d, a, far], dev(y, to, c, x))

    def arrival(cc, a, far, d):
        ref = piece(cc, a, at_distance(far, d))
        return remote(ref, ref, rs.at[d, a, far], rr.at[d, a, far], dev(y, z, c, x))

    def to_core0(a, zz):
        return remote(ring.at[a, :, zz], gat.at[a, :, zz], ffs.at[a, zz], ffr.at[a, zz], dev(y, z, 0, x))

    def to_head4(b, zz):
        ref = gat.at[2 * b : 2 * b + 2, y, zz]
        return remote(ref, ref, qfs.at[b, zz], fr.at[b, y, zz], dev(0, z, 1, x))

    def pass_on(a, zz):
        if a in (0, 3):

            @pl.when(y != 0)
            def _():
                to_head4(a // 3, zz).start()
        else:
            to_core0(a - 1, zz).start()

    def hops(cc, a, level):
        for near, far in paths[cc][level]:
            for d in (0, 1):
                if near > 0:
                    arrival(cc, a, near, d).wait_recv()
                if far <= most_far[d]:
                    hop(cc, a, near, far, d).start()
                if cc == 1:
                    pass_on(a, at_distance(near, d)) if near > 0 or (d == 0 and far == 1) else None

    def all_hops(cc, levels):
        for level in levels:
            for a in range(pieces[cc]):
                hops(cc, a, level)

    def last_arrivals(cc):
        starts = [near for level in paths[cc] for near, _ in level]
        for a in range(pieces[cc]):
            for far in range(1, 9):
                for d in (0, 1):
                    if far not in starts and far <= most_far[d]:
                        arrival(cc, a, far, d).wait_recv()
                        if cc == 1:
                            pass_on(a, at_distance(far, d))

    def first_hops(cc):
        for p in range(8):
            yy, pc = p // 2, p % 2
            got = gat.at[2:4, yy, z, pl.ds(pc * CAP, CAP), :] if cc == 0 else ring.at[:, yy, z, pl.ds(pc * CAP, CAP), :]

            @pl.when(p != me)
            def _():
                remote(got, got, p1s.at[0, 0], p1r.at[p], dev(yy, z, pc, x)).wait_recv()

        if cc == 1:
            got = gat.at[:, y, z, pl.ds(0, CAP), :]
            remote(got, got, qr_s, qr_r, dev(y, z, 0, x)).wait_recv()
            all_hops(1, (0,))
        else:
            hops(0, 0, 0)
            hops(0, 1, 0)

    @pl.when(c == 0)
    def _():
        first_hops(0)
        for p in range(8):

            @pl.when(p != me)
            def _():
                remote(ltile, lplane.at[p], ls.at[0], lr.at[p], dev(p // 2, z, p % 2, x)).wait_recv()

        total = jnp.zeros((16, 128), F32)
        for p in range(8):
            total = total + lplane[p].astype(F32)
        lall[z] = total.astype(BF16)
        hops(0, 2, 0)

    @pl.when(c == 1)
    def _():
        first_hops(1)

    sub = iota((128, 128), 0)
    lane = iota((128, 128), 1)

    @pl.when(is_owner)
    def _():
        before = (sub < lane).astype(BF16)
        base = jnp.zeros((128, 1), F32)
        for t in range(16):
            line = own_ref[t : t + 1, :]
            names = (sub == line).astype(F32)
            count = dot(names.astype(BF16), before, 1, 0)
            rank = jnp.sum(names * (count + base), axis=0, keepdims=True)
            base = base + jnp.sum(names, axis=1, keepdims=True)
            slot[t : t + 1, :] = line.astype(F32) * 16.0 + rank
        slot[16:, :] = jnp.zeros((112, 128), F32)

    @pl.when(c == 0)
    def _():
        all_hops(0, (1,))

    @pl.when(c == 1)
    def _():
        all_hops(1, (1,))

    @pl.when(is_owner)
    def _():
        slot_col = jnp.transpose(slot[...])
        own_slot = ((sub // 32) * 512 + z * 32 + sub % 32).astype(F32)
        for t in range(16):
            cols = slice(t * 128, (t + 1) * 128)
            sel[:, cols] = (own_slot == slot[t : t + 1, :]).astype(BF16)
            column = jnp.broadcast_to(slot_col[:, t : t + 1], (128, 128))
            for u in range(16):
                pt[cols, u * 128 : (u + 1) * 128] = (column == (lane + u * 128).astype(F32)).astype(BF16)

    @pl.when(c == 0)
    def _():
        all_hops(0, range(2, len(paths[0])))

    @pl.when(c == 1)
    def _():
        all_hops(1, range(2, len(paths[1])))
        last_arrivals(1)

    def window(zz):
        return pl.ds(pl.multiple_of(x * 1280 + (zz * 80 // 128) * 128, 128), 256)

    xt_rows = pl.ds(pl.multiple_of(z * 32 + c * CAP, CAP), CAP)

    def to_column(i):
        zz = (z + i) % NZ
        return remote(xc.at[:, window(zz)], xt.at[xt_rows, :], xts.at[i], xtr.at[c, z], dev(y, zz, 0, x))

    late = (3, 8, 13)

    @pl.when(c == 0)
    def _():
        for i in range(1, NZ):
            if i not in late:
                to_column(i).start()
        xt[xt_rows, :] = xc[:, window(z)]

    @pl.when(c == 1)
    def _():
        for i in range(NZ):
            to_column(i).start()

    def to_sibling():
        return remote(lsum, lsum, dls, dlr, dev(0, z, 1, x))

    def all_rows(a):
        return gat[a].reshape(ROWS, HD)

    def to_slot_owner(i):
        yy, cc = plane[i - 1]
        theirs = pl.ds(pl.multiple_of(yy * 32 + cc * CAP, CAP), CAP)
        return remote(
            ob.at[:, theirs, :],
            outs.at[:, :, pl.ds(pl.multiple_of(head * HD, HD), HD)],
            outsem_s.at[i], outsem_r.at[head], dev(yy, z, cc, x),
        )

    def to_rows(t, k):
        return remote(gl.at[t], lgx.at[mine], gs.at[t, k], gr.at[mine], dev(t, z, 0, (x + k) % NX))

    def each_rows(t, act):
        for k in range(NX):
            if k == 0:

                @pl.when((y != t) | (c != 0))
                def _():
                    act(to_rows(t, k))
            else:
                act(to_rows(t, k))

    @pl.when(is_owner)
    def _():
        @pl.when(c == 0)
        def _():
            for zz in range(NZ):
                for a in range(2):
                    to_core0(a, zz).wait_recv()

        @pl.when(c == 1)
        def _():
            for yy in range(1, 4):
                for zz in range(NZ):
                    ref = gat.at[0:2, yy, zz]
                    remote(ref, ref, qfs.at[0, 0], fr.at[0, yy, zz], dev(yy, z, 1, x)).wait_recv()

        for t in range(4):
            cols = slice(t * 512, (t + 1) * 512)
            q_block = gat[Q, t].reshape(512, HD)
            most = jnp.full((1, 512), -jnp.inf, F32)
            for u in range(t + 1):
                score = dot(gat[K, u].reshape(512, HD), q_block, 1, 1)
                if u == t:
                    score = jnp.where(iota((512, 512), 0) <= iota((512, 512), 1), score, -jnp.inf)
                st[u * 512 : (u + 1) * 512, :] = score
                most = jnp.maximum(most, jnp.max(score, axis=0, keepdims=True))
            total = jnp.zeros((1, 512), F32)
            for u in range(t + 1):
                keys = slice(u * 512, (u + 1) * 512)
                weight = jnp.exp2((st[keys, :] - most) * SCALE2)
                total = total + jnp.sum(weight, axis=0, keepdims=True)
                wt[keys, cols] = weight.astype(BF16)
            rows[0:1, cols] = most * SCALE2 + jnp.log2(total)
            rows[3:4, cols] = 1.0 / total

        @pl.when(c == 0)
        def _():
            last_arrivals(0)
            for i in late:
                to_column(i).start()
            total = jnp.zeros((16, 128), F32)
            for zz in range(NZ):
                total = total + lall[zz].astype(F32)
            lsum[...] = total

            @pl.when(y == 0)
            def _():
                to_sibling().start()

        @pl.when(c == 1)
        def _():
            to_sibling().wait_recv()
            for yy in range(1, 4):
                for zz in range(NZ):
                    ref = gat.at[2:4, yy, zz]
                    remote(ref, ref, qfs.at[0, 0], fr.at[1, yy, zz], dev(yy, z, 1, x)).wait_recv()

        for t in range(16):
            cols = slice(t * 128, (t + 1) * 128)
            rows[2:3, cols] = jax.nn.sigmoid(lsum[t : t + 1, :])

        vt[...] = jnp.transpose(all_rows(V))
        for t in range(4):
            part_rows = slice(t * 512, (t + 1) * 512)
            block = dot(pt[part_rows, :], all_rows(G), 1, 0)
            gc[part_rows, :] = block.astype(BF16)
            gct[:, part_rows] = jnp.transpose(block.astype(BF16))
        pl.semaphore_wait(xready, 3)
        for t in (3, 2, 1, 0):
            cols = slice(t * 512, (t + 1) * 512)
            n = (t + 1) * 512
            ctx = dot(vt[:, :n], wt[:n, cols], 1, 0)
            gate_part = jnp.sum(ctx * gct[:, cols].astype(F32), axis=0, keepdims=True) * rows[3:4, cols]
            gating = rows[2:3, cols]
            rows[1:2, cols] = gating * gate_part
            logit_grad = gate_part * gating * (1.0 - gating)
            for u in range(4):
                gl[t, u : u + 1, :] = logit_grad[:, u * 128 : (u + 1) * 128]
            gl[t, 4:8, :] = jnp.zeros((4, 128), F32)
            each_rows(t, lambda copy: copy.start())

        @pl.when(c == 0)
        def _():
            lgx[mine] = gl[y]

        for t in range(16):
            cols = slice(t * 128, (t + 1) * 128)
            row16 = iota((16, 128), 0)
            lane16 = iota((16, 128), 1)
            value = jnp.where(row16 == 0, t * 8 + lane16 // 16, jnp.where(row16 == 1, lane16 % 16, 0))
            ownx[:, cols] = jnp.where(row16 == 2, lsum[t : t + 1, :], value.astype(F32)).astype(BF16)
        own = dot(sel[...], ownx[...], 1, 1)
        own_j = own[:, 0:1] * 16.0 + own[:, 1:2]
        own_j_row = jnp.transpose(jnp.broadcast_to(own_j, (128, 128)))[0:1]
        own_gate = jax.nn.sigmoid(jnp.transpose(jnp.broadcast_to(own[:, 2:3], (128, 128)))[0:1])

        selw = sel[...]
        q_own = dot(selw, all_rows(Q), 1, 0).astype(BF16)
        k_own = dot(selw, all_rows(K), 1, 0).astype(BF16)

        score = dot(all_rows(K), q_own, 1, 1)
        score = jnp.where(iota((ROWS, 128), 0).astype(F32) <= own_j_row, score, -jnp.inf)
        most = jnp.max(score, axis=0, keepdims=True)
        weight = jnp.exp2((score - most) * SCALE2)
        wo[...] = (weight * (1.0 / jnp.sum(weight, axis=0, keepdims=True))).astype(BF16)

        score = dot(k_own, all_rows(Q), 1, 1) * SCALE2
        causal = iota((128, ROWS), 1).astype(F32) >= own_j
        w2[...] = jnp.exp2(jnp.where(causal, score - rows[0:1, :], -jnp.inf)).astype(BF16)

        v_own = dot(selw, all_rows(V), 1, 0).astype(BF16)
        g_own = gat[G, :, z].reshape(128, HD)
        ctx = dot(vt[...], wo[...], 1, 0)
        g_own_t = jnp.transpose(g_own.astype(F32))
        delta = jnp.sum(ctx * g_own_t, axis=0, keepdims=True) * own_gate
        ob[0] = jnp.transpose(ctx * own_gate).astype(BF16)
        prob_grad = dot(all_rows(V), g_own, 1, 1) * own_gate
        score_grad = (wo[...].astype(F32) * (prob_grad - delta)).astype(BF16)
        ob[1] = (dot(score_grad, all_rows(K), 0, 0) * SCALE).astype(BF16)

        weight = w2[...].astype(F32)
        prob_grad = dot(v_own, gc[...], 1, 1) * rows[2:3, :]
        score_grad = (weight * (prob_grad - rows[1:2, :])).astype(BF16)
        ob[2] = (dot(score_grad, all_rows(Q), 1, 0) * SCALE).astype(BF16)
        ob[3] = dot((weight * rows[2:3, :]).astype(BF16), gc[...], 1, 0).astype(BF16)
        for i in range(1, 8):
            to_slot_owner(i).start()
        here = pl.ds(pl.multiple_of(y * 32 + c * CAP, CAP), CAP)
        outs[:, :, pl.ds(pl.multiple_of(head * HD, HD), HD)] = ob[:, here, :]

    @pl.when(jnp.logical_not(is_owner))
    def _():
        pl.semaphore_wait(xready, 3)

    def to_part(xx, cc):
        return remote(part, pr.at[y], prs.at[xx, cc], prr.at[y], dev(x, z, cc, xx))

    def each_part(act):
        for xx in range(4):
            for cc in range(2):

                @pl.when((y != x) | (x != xx) | (cc != 0))
                def _():
                    act(to_part(xx, cc))

    @pl.when(c == 0)
    def _():
        for cc in range(2):
            for i in range(1 - cc, NZ):
                zz = (z + i) % NZ
                got = xt.at[pl.ds(pl.multiple_of(zz * 32 + cc * CAP, CAP), CAP), :]
                remote(got, got, xts.at[0], xtr.at[cc, zz], dev(y, zz, cc, x)).wait_recv()
        for p in range(20):
            xx, h = p // 5, p % 5
            yy, cc = (h, 0) if h < 4 else (0, 1)

            @pl.when(p != mine)
            def _():
                remote(lgx.at[p], lgx.at[p], gs.at[0, 0], gr.at[p], dev(yy, z, cc, xx)).wait_recv()

        logit_grad = lgx[0]
        for p in range(1, 20):
            logit_grad = logit_grad + lgx[p]
        total = jnp.zeros((8, 256), F32)
        for t in range(4):
            line = jnp.broadcast_to(logit_grad[t : t + 1, :], (8, 128))
            total = total + lax.dot_general(
                line, xt[t * 128 : (t + 1) * 128, :].astype(F32), (((1,), (0,)), ((), ())),
                precision=lax.Precision.HIGHEST, preferred_element_type=F32,
            )
        part[...] = total
        each_part(lambda copy: copy.start())

        @pl.when(y == x)
        def _():
            pr[y] = part[...]

    for p in range(4):

        @pl.when((p != y) | (y != x) | (c != 0))
        def _():
            remote(pr.at[p], pr.at[p], prs.at[0, 0], prr.at[p], dev(p, z, 0, y)).wait_recv()

    total = pr[0] + pr[1] + pr[2] + pr[3]
    offset = (z * 80) % 128 + c * 40
    router_ref[...] = pltpu.roll(total, (256 - offset) % 256, 1)[:, :128]

    for h in range(5):
        yy, cc = (h, 0) if h < 4 else (0, 1)

        @pl.when((yy != y) | (cc != c))
        def _():
            got = outs.at[:, :, pl.ds(h * HD, HD)]
            remote(got, got, outsem_s.at[0], outsem_r.at[h], dev(yy, z, cc, x)).wait_recv()

    out_ref[...] = outs[...]

    for h in range(4):
        for cc in range(2):

            @pl.when((c != cc) | (y != h))
            def _():
                to_head(h, cc).wait_send()

        @pl.when((c != 0) | (y != h))
        def _():
            to_logit(h).wait_send()

    def sent(cc):
        for a in range(pieces[cc]):
            for level in paths[cc]:
                for near, far in level:
                    for d in (0, 1):
                        if far <= most_far[d]:
                            hop(cc, a, near, far, d).wait_send()

    @pl.when(c == 0)
    def _():
        to_quarter().wait_send()
        sent(0)

        @pl.when(y == 0)
        def _():
            to_sibling().wait_send()

    @pl.when(c == 1)
    def _():
        sent(1)
        for zz in range(NZ):
            to_core0(0, zz).wait_send()
            to_core0(1, zz).wait_send()

        @pl.when(y != 0)
        def _():
            for zz in range(NZ):
                to_head4(0, zz).wait_send()
                to_head4(1, zz).wait_send()

    for i in range(1, NZ):
        to_column(i).wait_send()

    @pl.when(c == 1)
    def _():
        to_column(0).wait_send()

    @pl.when(is_owner)
    def _():
        for i in range(1, 8):
            to_slot_owner(i).wait_send()
        for t in range(4):
            each_rows(t, lambda copy: copy.wait_send())

    @pl.when(c == 0)
    def _():
        each_part(lambda copy: copy.wait_send())


def body(stream, queries, keys, values, router_weight, chosen, owner, grad_out):
    vmem = pl.BlockSpec(memory_space=pltpu.VMEM)
    hbm = pl.BlockSpec(memory_space=pl.ANY)
    dma = pltpu.SemaphoreType.DMA
    scratch = [
        pltpu.VMEM((128, 5120), BF16),
        pltpu.VMEM((128, 5 * HD), BF16),
        pltpu.VMEM((128, 5 * HD), BF16),
        pltpu.VMEM((128, 5 * HD), BF16),
        pltpu.VMEM((5120,), BF16),
        pltpu.VMEM((16, 128), jnp.int32),
        pltpu.VMEM((4, CAP, 5 * HD), BF16),
        pltpu.VMEM((4, NY, NZ, 32, HD), BF16),
        pltpu.VMEM((2, NY, NZ, 32, HD), BF16),
        pltpu.VMEM((CAP, 5248), BF16),
        pltpu.VMEM((512, 256), BF16),
        pltpu.VMEM((16, 128), BF16),
        pltpu.VMEM((8, 16, 128), BF16),
        pltpu.VMEM((NZ, 16, 128), BF16),
        pltpu.VMEM((16, 128), F32),
        pltpu.VMEM((128, 128), F32),
        pltpu.VMEM((ROWS, ROWS), BF16),
        pltpu.VMEM((128, ROWS), BF16),
        pltpu.VMEM((16, ROWS), BF16),
        pltpu.VMEM((ROWS, 512), F32),
        pltpu.VMEM((ROWS, ROWS), BF16),
        pltpu.VMEM((ROWS, 128), BF16),
        pltpu.VMEM((128, ROWS), BF16),
        pltpu.VMEM((HD, ROWS), BF16),
        pltpu.VMEM((HD, ROWS), BF16),
        pltpu.VMEM((ROWS, HD), BF16),
        pltpu.VMEM((8, ROWS), F32),
        pltpu.VMEM((4, 128, HD), BF16),
        pltpu.VMEM((4, CAP, 5 * HD), BF16),
        pltpu.VMEM((NY, 8, 128), F32),
        pltpu.VMEM((20, 8, 128), F32),
        pltpu.VMEM((8, 256), F32),
        pltpu.VMEM((4, 8, 256), F32),
        dma((7,)), dma((4, 2)), dma((8,)), dma, dma, dma((4,)), dma((8,)),
        dma((2, 4, 9)), dma((2, 4, 9)), dma((2, 16)), dma((2, 16)), dma((2, 16)), dma((2, 4, 16)), dma, dma,
        dma((16,)), dma((2, 16)), dma((8,)), dma((5,)), dma((4, 4)), dma((20,)), dma((4, 2)), dma((4,)),
        pltpu.SemaphoreType.REGULAR,
    ]
    out, router = pl.pallas_call(
        kernel,
        out_shape=(
            jax.ShapeDtypeStruct((4, CAP, 5 * HD), BF16),
            jax.ShapeDtypeStruct((8, 128), F32),
        ),
        in_specs=[pl.BlockSpec(memory_space=pltpu.SMEM)] + [hbm] * 7,
        out_specs=(vmem,) * 2,
        scratch_shapes=scratch,
        compiler_params=pltpu.CompilerParams(
            collective_id=0, has_side_effects=True, vmem_limit_bytes=56 * 2**20
        ),
        name="routed_attention",
    )(
        chosen, owner.reshape(16, 128), router_weight,
        queries, keys, values, grad_out, stream,
    )

    def split(out_ref, router_in, *refs):
        for i in range(4):
            refs[i][...] = out_ref[i]
        refs[4][...] = router_in[0, :40]

    wide = jax.ShapeDtypeStruct((CAP, 5 * HD), BF16)
    return pl.pallas_call(
        split,
        out_shape=(wide, wide, wide, wide, jax.ShapeDtypeStruct((40,), F32)),
        in_specs=[vmem] * 2,
        out_specs=(vmem,) * 5,
        name="split_outputs",
    )(out, router)


def solution(mesh):
    return jax.shard_map(
        body,
        mesh=mesh,
        in_specs=(
            P("seq", None),
            P("seq", "head"),
            P("seq", "head"),
            P("seq", "head"),
            P(),
            P(),
            P(),
            P("seq", "head"),
        ),
        out_specs=(
            P("seq", "head"),
            P("seq", "head"),
            P("seq", "head"),
            P("seq", "head"),
            P("seq"),
        ),
        check_vma=False,
    )
```

```python
import jax
import jax.numpy as jnp
from jax import lax
from jax.experimental import pallas as pl
from jax.experimental.pallas import tpu as pltpu
from jax.sharding import PartitionSpec as P

NY, NZ, NX = 4, 16, 4
CAP = 16
HD = 128
ROWS = 2048
SCALE = HD**-0.5
SCALE2 = SCALE * 1.4426950408889634
MESH = pl.DeviceIdType.MESH
Q, K, G, V = 0, 1, 2, 3
F32, BF16 = jnp.float32, jnp.bfloat16


def dot(a, b, ca, cb):
    return lax.dot_general(a, b, (((ca,), (cb,)), ((), ())), preferred_element_type=F32)


def iota(shape, dim):
    return lax.broadcasted_iota(jnp.int32, shape, dim)


def kernel(
    chosen_ref, owner_in, weight_in, q_in, k_in, v_in, g_in, stream_in,
    out_ref, router_ref,
    xs, qin, kin, vin, win, own_ref, pk, gat, ring, xc, xt, ltile, lplane, lall, lsum,
    slot, pt, sel, ownx, st, wt, wo, w2, vt, gct, gc, rows, ob, outs,
    gl, lgx, part, pr,
    sem_in, p1s, p1r, qr_s, qr_r, ls, lr, rs, rr, ffs, ffr, qfs, fr, dls, dlr, xts, xtr,
    outsem_s, outsem_r, gs, gr, prs, prr, xready,
):
    seq, x = lax.axis_index("seq"), lax.axis_index("head")
    y, z, c = seq // 32, (seq // 2) % NZ, seq % 2
    me = y * 2 + c
    is_owner = (c == 0) | (y == 0)
    head = y * (1 - c) + 4 * c
    mine = x * 5 + head

    def dev(yy, zz, cc, xx):
        return (yy * 32 + zz * 2 + cc, xx)

    def remote(src, dst, ss, rsem, target):
        return pltpu.make_async_remote_copy(
            src_ref=src, dst_ref=dst, send_sem=ss, recv_sem=rsem, device_id=target, device_id_type=MESH
        )

    def signal(sem, target):
        pl.semaphore_signal(sem, inc=1, device_id=target, device_id_type=MESH)

    loads = [
        pltpu.make_async_copy(src, dst, sem_in.at[i])
        for i, (src, dst) in enumerate(
            [
                (q_in, qin), (k_in, kin), (v_in, vin), (g_in, pk.at[G]),
                (stream_in, xs), (weight_in, win), (owner_in, own_ref),
            ]
        )
    ]
    for load in loads[:4]:
        load.start()

    plane = []
    for i in range(1, 8):
        p = (me + i) % 8
        plane.append((p // 2, p % 2))
    peers = [dev(yy, z, cc, x) for yy, cc in plane]
    peers += [dev(y, (z + i) % NZ, c, x) for i in (1, NZ - 1, 4, NZ - 4)]
    peers += [dev(y, z, c, (x + i) % NX) for i in range(1, NX)]
    barrier = pltpu.get_barrier_semaphore()
    for p in peers:
        signal(barrier, p)
    for load in loads[4:]:
        load.start()

    token = jnp.zeros((CAP, 128), jnp.int32)
    for r in range(CAP):
        token = jnp.where(iota((CAP, 128), 0) == r, chosen_ref[seq * CAP + r] - seq * 128, token)
    pick = (token == iota((CAP, 128), 1)).astype(BF16)
    for load in loads[:4]:
        load.wait()
    pk[Q] = dot(pick, qin[...], 1, 0).astype(BF16)
    pk[K] = dot(pick, kin[...], 1, 0).astype(BF16)
    pk[V] = dot(pick, vin[...], 1, 0).astype(BF16)
    pl.semaphore_wait(barrier, len(peers))

    my_rows = pl.ds(pl.multiple_of(c * CAP, CAP), CAP)

    def to_head(h, cc):
        src = pk.at[2 - 2 * cc : 4 - 2 * cc, :, pl.ds(h * HD, HD)]
        dst = gat.at[2:4, y, z, my_rows, :] if cc == 0 else ring.at[:, y, z, my_rows, :]
        return remote(src, dst, p1s.at[h, cc], p1r.at[me], dev(h, z, cc, x))

    def to_quarter():
        src = pk.at[:, :, pl.ds(4 * HD, HD)]
        return remote(src, gat.at[:, y, z, my_rows, :], qr_s, qr_r, dev(y, z, 1, x))

    def to_logit(h):
        return remote(ltile, lplane.at[me], ls.at[h], lr.at[me], dev(h, z, 0, x))

    for h in range(4):
        for cc in range(2):
            here = (c == cc) & (y == h)

            @pl.when(jnp.logical_not(here))
            def _():
                to_head(h, cc).start()

    @pl.when(c == 0)
    def _():
        to_quarter().start()
        gat[2:4, y, z, my_rows, :] = pk[2:4, :, pl.ds(pl.multiple_of(y * HD, HD), HD)]

    @pl.when(c == 1)
    def _():
        ring[:, y, z, my_rows, :] = pk[0:2, :, pl.ds(pl.multiple_of(y * HD, HD), HD)]
        gat[:, y, z, my_rows, :] = pk[:, :, 4 * HD : 5 * HD]

    for load in loads[4:]:
        load.wait()
    for t in range(5):
        cols = slice(t * 1024, (t + 1) * 1024)
        xc[:, cols] = dot(pick, xs[:, cols], 1, 0).astype(BF16)
    xc[:, 5120:] = jnp.zeros((CAP, 128), BF16)
    logit = jnp.sum(xc[:, :5120].astype(F32) * win[...].reshape(1, 5120).astype(F32), axis=1, keepdims=True)
    spread = jnp.where(
        iota((CAP, 128), 1) == (seq % 8) * CAP + iota((CAP, 128), 0), logit, jnp.zeros((), F32)
    )
    line = jnp.sum(spread, axis=0, keepdims=True)
    ltile[...] = jnp.where(iota((16, 128), 0) == seq // 8, line, jnp.zeros((), F32)).astype(BF16)

    for h in range(4):

        @pl.when((c != 0) | (y != h))
        def _():
            to_logit(h).start()

    @pl.when(c == 0)
    def _():
        lplane[me] = ltile[...]

    for i in range(1, NX):
        signal(xready, dev(y, z, c, (x + i) % NX))

    paths = (
        (((0, 1), (0, 4)), ((1, 2), (4, 5)), ((2, 3), (5, 6)), ((6, 7),), ((7, 8),)),
        (((0, 1),), ((1, 2),), ((2, 3),), ((3, 4),), ((4, 5),), ((5, 6),), ((6, 7),), ((7, 8),)),
    )
    most_far = (8, 7)
    pieces = (3, 4)

    def piece(cc, a, zz):
        if cc == 0:
            return lall.at[zz] if a == 2 else gat.at[2 + a, :, zz]
        return gat.at[0:2, y, zz] if a == 0 else gat.at[2:4, y, zz] if a == 3 else ring.at[a - 1, :, zz]

    def at_distance(s, d):
        return (z - s + 2 * NZ) % NZ if d == 0 else (z + s) % NZ

    def hop(cc, a, near, far, d):
        ref = piece(cc, a, at_distance(near, d))
        to = (z + far - near) % NZ if d == 0 else (z + near - far + NZ) % NZ
        return remote(ref, ref, rs.at[d, a, far], rr.at[d, a, far], dev(y, to, c, x))

    def arrival(cc, a, far, d):
        ref = piece(cc, a, at_distance(far, d))
        return remote(ref, ref, rs.at[d, a, far], rr.at[d, a, far], dev(y, z, c, x))

    def to_core0(a, zz):
        return remote(ring.at[a, :, zz], gat.at[a, :, zz], ffs.at[a, zz], ffr.at[a, zz], dev(y, z, 0, x))

    def to_head4(b, zz):
        ref = gat.at[2 * b : 2 * b + 2, y, zz]
        return remote(ref, ref, qfs.at[b, zz], fr.at[b, y, zz], dev(0, z, 1, x))

    def pass_on(a, zz):
        if a in (0, 3):

            @pl.when(y != 0)
            def _():
                to_head4(a // 3, zz).start()
        else:
            to_core0(a - 1, zz).start()

    def hops(cc, a, level):
        for near, far in paths[cc][level]:
            for d in (0, 1):
                if near > 0:
                    arrival(cc, a, near, d).wait_recv()
                if far <= most_far[d]:
                    hop(cc, a, near, far, d).start()
                if cc == 1:
                    pass_on(a, at_distance(near, d)) if near > 0 or (d == 0 and far == 1) else None

    def all_hops(cc, levels):
        for level in levels:
            for a in range(pieces[cc]):
                hops(cc, a, level)

    def last_arrivals(cc):
        starts = [near for level in paths[cc] for near, _ in level]
        for a in range(pieces[cc]):
            for far in range(1, 9):
                for d in (0, 1):
                    if far not in starts and far <= most_far[d]:
                        arrival(cc, a, far, d).wait_recv()
                        if cc == 1:
                            pass_on(a, at_distance(far, d))

    def first_hops(cc):
        for p in range(8):
            yy, pc = p // 2, p % 2
            got = gat.at[2:4, yy, z, pl.ds(pc * CAP, CAP), :] if cc == 0 else ring.at[:, yy, z, pl.ds(pc * CAP, CAP), :]

            @pl.when(p != me)
            def _():
                remote(got, got, p1s.at[0, 0], p1r.at[p], dev(yy, z, pc, x)).wait_recv()

        if cc == 1:
            got = gat.at[:, y, z, pl.ds(0, CAP), :]
            remote(got, got, qr_s, qr_r, dev(y, z, 0, x)).wait_recv()
            all_hops(1, (0,))
        else:
            hops(0, 0, 0)
            hops(0, 1, 0)

    @pl.when(c == 0)
    def _():
        first_hops(0)
        for p in range(8):

            @pl.when(p != me)
            def _():
                remote(ltile, lplane.at[p], ls.at[0], lr.at[p], dev(p // 2, z, p % 2, x)).wait_recv()

        total = jnp.zeros((16, 128), F32)
        for p in range(8):
            total = total + lplane[p].astype(F32)
        lall[z] = total.astype(BF16)
        hops(0, 2, 0)

    @pl.when(c == 1)
    def _():
        first_hops(1)

    sub = iota((128, 128), 0)
    lane = iota((128, 128), 1)

    @pl.when(is_owner)
    def _():
        before = (sub < lane).astype(BF16)
        base = jnp.zeros((128, 1), F32)
        for t in range(16):
            line = own_ref[t : t + 1, :]
            names = (sub == line).astype(F32)
            count = dot(names.astype(BF16), before, 1, 0)
            rank = jnp.sum(names * (count + base), axis=0, keepdims=True)
            base = base + jnp.sum(names, axis=1, keepdims=True)
            slot[t : t + 1, :] = line.astype(F32) * 16.0 + rank
        slot[16:, :] = jnp.zeros((112, 128), F32)

    @pl.when(c == 0)
    def _():
        all_hops(0, (1,))

    @pl.when(c == 1)
    def _():
        all_hops(1, (1,))

    @pl.when(is_owner)
    def _():
        slot_col = jnp.transpose(slot[...])
        own_slot = ((sub // 32) * 512 + z * 32 + sub % 32).astype(F32)
        for t in range(16):
            cols = slice(t * 128, (t + 1) * 128)
            sel[:, cols] = (own_slot == slot[t : t + 1, :]).astype(BF16)
            column = jnp.broadcast_to(slot_col[:, t : t + 1], (128, 128))
            for u in range(16):
                pt[cols, u * 128 : (u + 1) * 128] = (column == (lane + u * 128).astype(F32)).astype(BF16)

    @pl.when(c == 0)
    def _():
        all_hops(0, range(2, len(paths[0])))

    @pl.when(c == 1)
    def _():
        all_hops(1, range(2, len(paths[1])))
        last_arrivals(1)

    def window(zz):
        return pl.ds(pl.multiple_of(x * 1280 + (zz * 80 // 128) * 128, 128), 256)

    xt_rows = pl.ds(pl.multiple_of(z * 32 + c * CAP, CAP), CAP)

    def to_column(i):
        zz = (z + i) % NZ
        return remote(xc.at[:, window(zz)], xt.at[xt_rows, :], xts.at[i], xtr.at[c, z], dev(y, zz, 0, x))

    late = (3, 8, 13)

    @pl.when(c == 0)
    def _():
        for i in range(1, NZ):
            if i not in late:
                to_column(i).start()
        xt[xt_rows, :] = xc[:, window(z)]

    @pl.when(c == 1)
    def _():
        for i in range(NZ):
            to_column(i).start()

    def to_sibling():
        return remote(lsum, lsum, dls, dlr, dev(0, z, 1, x))

    def all_rows(a):
        return gat[a].reshape(ROWS, HD)

    def to_slot_owner(i):
        yy, cc = plane[i - 1]
        theirs = pl.ds(pl.multiple_of(yy * 32 + cc * CAP, CAP), CAP)
        return remote(
            ob.at[:, theirs, :],
            outs.at[:, :, pl.ds(pl.multiple_of(head * HD, HD), HD)],
            outsem_s.at[i], outsem_r.at[head], dev(yy, z, cc, x),
        )

    def to_rows(t, k):
        return remote(gl.at[t], lgx.at[mine], gs.at[t, k], gr.at[mine], dev(t, z, 0, (x + k) % NX))

    def each_rows(t, act):
        for k in range(NX):
            if k == 0:

                @pl.when((y != t) | (c != 0))
                def _():
                    act(to_rows(t, k))
            else:
                act(to_rows(t, k))

    @pl.when(is_owner)
    def _():
        @pl.when(c == 0)
        def _():
            for zz in range(NZ):
                for a in range(2):
                    to_core0(a, zz).wait_recv()

        @pl.when(c == 1)
        def _():
            for yy in range(1, 4):
                for zz in range(NZ):
                    ref = gat.at[0:2, yy, zz]
                    remote(ref, ref, qfs.at[0, 0], fr.at[0, yy, zz], dev(yy, z, 1, x)).wait_recv()

        for t in range(8):
            cols = slice(t * 256, (t + 1) * 256)
            n = t * 256
            half = slice(t % 2 * 8, t % 2 * 8 + 8)
            q_block = gat[Q, t // 2, half].reshape(256, HD)
            if t:
                st[:n, :] = dot(gat[K].reshape(ROWS, HD)[:n], q_block, 1, 1)
            score = dot(gat[K, t // 2, half].reshape(256, HD), q_block, 1, 1)
            st[n : n + 256, :] = jnp.where(iota((256, 256), 0) <= iota((256, 256), 1), score, -jnp.inf)
            most = jnp.full((1, 256), -jnp.inf, F32)
            for u in range(t + 1):
                most = jnp.maximum(most, jnp.max(st[u * 256 : (u + 1) * 256, :], axis=0, keepdims=True))
            total = jnp.zeros((1, 256), F32)
            for u in range(t + 1):
                keys = slice(u * 256, (u + 1) * 256)
                weight = jnp.exp2((st[keys, :] - most) * SCALE2)
                total = total + jnp.sum(weight, axis=0, keepdims=True)
                wt[keys, cols] = weight.astype(BF16)
            if t % 2 == 0:
                wt[n + 256 : n + 512, cols] = jnp.zeros((256, 256), BF16)
            rows[0:1, cols] = most * SCALE2 + jnp.log2(total)
            rows[3:4, cols] = 1.0 / total

        @pl.when(c == 0)
        def _():
            last_arrivals(0)
            for i in late:
                to_column(i).start()
            total = jnp.zeros((16, 128), F32)
            for zz in range(NZ):
                total = total + lall[zz].astype(F32)
            lsum[...] = total

            @pl.when(y == 0)
            def _():
                to_sibling().start()

        @pl.when(c == 1)
        def _():
            to_sibling().wait_recv()
            for yy in range(1, 4):
                for zz in range(NZ):
                    ref = gat.at[2:4, yy, zz]
                    remote(ref, ref, qfs.at[0, 0], fr.at[1, yy, zz], dev(yy, z, 1, x)).wait_recv()

        for t in range(16):
            cols = slice(t * 128, (t + 1) * 128)
            rows[2:3, cols] = jax.nn.sigmoid(lsum[t : t + 1, :])

        vt[...] = jnp.transpose(all_rows(V))
        for t in range(4):
            part_rows = slice(t * 512, (t + 1) * 512)
            block = dot(pt[part_rows, :], all_rows(G), 1, 0)
            gc[part_rows, :] = block.astype(BF16)
            gct[:, part_rows] = jnp.transpose(block.astype(BF16))
        pl.semaphore_wait(xready, 3)
        for t in (3, 2, 1, 0):
            cols = slice(t * 512, (t + 1) * 512)
            n = (t + 1) * 512
            ctx = dot(vt[:, :n], wt[:n, cols], 1, 0)
            gate_part = jnp.sum(ctx * gct[:, cols].astype(F32), axis=0, keepdims=True) * rows[3:4, cols]
            gating = rows[2:3, cols]
            rows[1:2, cols] = gating * gate_part
            logit_grad = gate_part * gating * (1.0 - gating)
            for u in range(4):
                gl[t, u : u + 1, :] = logit_grad[:, u * 128 : (u + 1) * 128]
            gl[t, 4:8, :] = jnp.zeros((4, 128), F32)
            each_rows(t, lambda copy: copy.start())

        @pl.when(c == 0)
        def _():
            lgx[mine] = gl[y]

        for t in range(16):
            cols = slice(t * 128, (t + 1) * 128)
            row16 = iota((16, 128), 0)
            lane16 = iota((16, 128), 1)
            value = jnp.where(row16 == 0, t * 8 + lane16 // 16, jnp.where(row16 == 1, lane16 % 16, 0))
            ownx[:, cols] = jnp.where(row16 == 2, lsum[t : t + 1, :], value.astype(F32)).astype(BF16)
        own = dot(sel[...], ownx[...], 1, 1)
        own_j = own[:, 0:1] * 16.0 + own[:, 1:2]
        own_j_row = jnp.transpose(jnp.broadcast_to(own_j, (128, 128)))[0:1]
        own_gate = jax.nn.sigmoid(jnp.transpose(jnp.broadcast_to(own[:, 2:3], (128, 128)))[0:1])

        selw = sel[...]
        q_own = dot(selw, all_rows(Q), 1, 0).astype(BF16)
        k_own = dot(selw, all_rows(K), 1, 0).astype(BF16)

        score = dot(all_rows(K), q_own, 1, 1)
        score = jnp.where(iota((ROWS, 128), 0).astype(F32) <= own_j_row, score, -jnp.inf)
        most = jnp.max(score, axis=0, keepdims=True)
        weight = jnp.exp2((score - most) * SCALE2)
        wo[...] = (weight * (1.0 / jnp.sum(weight, axis=0, keepdims=True))).astype(BF16)

        score = dot(k_own, all_rows(Q), 1, 1) * SCALE2
        causal = iota((128, ROWS), 1).astype(F32) >= own_j
        w2[...] = jnp.exp2(jnp.where(causal, score - rows[0:1, :], -jnp.inf)).astype(BF16)

        v_own = dot(selw, all_rows(V), 1, 0).astype(BF16)
        g_own = gat[G, :, z].reshape(128, HD)
        ctx = dot(vt[...], wo[...], 1, 0)
        g_own_t = jnp.transpose(g_own.astype(F32))
        delta = jnp.sum(ctx * g_own_t, axis=0, keepdims=True) * own_gate
        ob[0] = jnp.transpose(ctx * own_gate).astype(BF16)
        prob_grad = dot(all_rows(V), g_own, 1, 1) * own_gate
        score_grad = (wo[...].astype(F32) * (prob_grad - delta)).astype(BF16)
        ob[1] = (dot(score_grad, all_rows(K), 0, 0) * SCALE).astype(BF16)

        weight = w2[...].astype(F32)
        prob_grad = dot(v_own, gc[...], 1, 1) * rows[2:3, :]
        score_grad = (weight * (prob_grad - rows[1:2, :])).astype(BF16)
        ob[2] = (dot(score_grad, all_rows(Q), 1, 0) * SCALE).astype(BF16)
        ob[3] = dot((weight * rows[2:3, :]).astype(BF16), gc[...], 1, 0).astype(BF16)
        for i in range(1, 8):
            to_slot_owner(i).start()
        here = pl.ds(pl.multiple_of(y * 32 + c * CAP, CAP), CAP)
        outs[:, :, pl.ds(pl.multiple_of(head * HD, HD), HD)] = ob[:, here, :]

    @pl.when(jnp.logical_not(is_owner))
    def _():
        pl.semaphore_wait(xready, 3)

    def to_part(xx, cc):
        return remote(part, pr.at[y], prs.at[xx, cc], prr.at[y], dev(x, z, cc, xx))

    def each_part(act):
        for xx in range(4):
            for cc in range(2):

                @pl.when((y != x) | (x != xx) | (cc != 0))
                def _():
                    act(to_part(xx, cc))

    @pl.when(c == 0)
    def _():
        for cc in range(2):
            for i in range(1 - cc, NZ):
                zz = (z + i) % NZ
                got = xt.at[pl.ds(pl.multiple_of(zz * 32 + cc * CAP, CAP), CAP), :]
                remote(got, got, xts.at[0], xtr.at[cc, zz], dev(y, zz, cc, x)).wait_recv()
        for p in range(20):
            xx, h = p // 5, p % 5
            yy, cc = (h, 0) if h < 4 else (0, 1)

            @pl.when(p != mine)
            def _():
                remote(lgx.at[p], lgx.at[p], gs.at[0, 0], gr.at[p], dev(yy, z, cc, xx)).wait_recv()

        logit_grad = lgx[0]
        for p in range(1, 20):
            logit_grad = logit_grad + lgx[p]
        total = jnp.zeros((8, 256), F32)
        for t in range(4):
            line = logit_grad[t : t + 1, :]
            high = line.astype(BF16).astype(F32)
            middle = (line - high).astype(BF16).astype(F32)
            row16 = iota((16, 128), 0)
            terms = jnp.where(row16 == 0, high, jnp.where(row16 == 1, middle, line - high - middle))
            terms = jnp.where(row16 < 3, terms, 0.0).astype(BF16)
            sums = jnp.sum(dot(terms, xt[t * 128 : (t + 1) * 128, :], 1, 0), axis=0, keepdims=True)
            total = total + jnp.broadcast_to(sums, (8, 256))
        part[...] = total
        each_part(lambda copy: copy.start())

        @pl.when(y == x)
        def _():
            pr[y] = part[...]

    for p in range(4):

        @pl.when((p != y) | (y != x) | (c != 0))
        def _():
            remote(pr.at[p], pr.at[p], prs.at[0, 0], prr.at[p], dev(p, z, 0, y)).wait_recv()

    total = pr[0] + pr[1] + pr[2] + pr[3]
    offset = (z * 80) % 128 + c * 40
    router_ref[...] = pltpu.roll(total, (256 - offset) % 256, 1)[:, :128]

    for h in range(5):
        yy, cc = (h, 0) if h < 4 else (0, 1)

        @pl.when((yy != y) | (cc != c))
        def _():
            got = outs.at[:, :, pl.ds(h * HD, HD)]
            remote(got, got, outsem_s.at[0], outsem_r.at[h], dev(yy, z, cc, x)).wait_recv()

    out_ref[...] = outs[...]

    for h in range(4):
        for cc in range(2):

            @pl.when((c != cc) | (y != h))
            def _():
                to_head(h, cc).wait_send()

        @pl.when((c != 0) | (y != h))
        def _():
            to_logit(h).wait_send()

    def sent(cc):
        for a in range(pieces[cc]):
            for level in paths[cc]:
                for near, far in level:
                    for d in (0, 1):
                        if far <= most_far[d]:
                            hop(cc, a, near, far, d).wait_send()

    @pl.when(c == 0)
    def _():
        to_quarter().wait_send()
        sent(0)

        @pl.when(y == 0)
        def _():
            to_sibling().wait_send()

    @pl.when(c == 1)
    def _():
        sent(1)
        for zz in range(NZ):
            to_core0(0, zz).wait_send()
            to_core0(1, zz).wait_send()

        @pl.when(y != 0)
        def _():
            for zz in range(NZ):
                to_head4(0, zz).wait_send()
                to_head4(1, zz).wait_send()

    for i in range(1, NZ):
        to_column(i).wait_send()

    @pl.when(c == 1)
    def _():
        to_column(0).wait_send()

    @pl.when(is_owner)
    def _():
        for i in range(1, 8):
            to_slot_owner(i).wait_send()
        for t in range(4):
            each_rows(t, lambda copy: copy.wait_send())

    @pl.when(c == 0)
    def _():
        each_part(lambda copy: copy.wait_send())


def body(stream, queries, keys, values, router_weight, chosen, owner, grad_out):
    vmem = pl.BlockSpec(memory_space=pltpu.VMEM)
    hbm = pl.BlockSpec(memory_space=pl.ANY)
    dma = pltpu.SemaphoreType.DMA
    scratch = [
        pltpu.VMEM((128, 5120), BF16),
        pltpu.VMEM((128, 5 * HD), BF16),
        pltpu.VMEM((128, 5 * HD), BF16),
        pltpu.VMEM((128, 5 * HD), BF16),
        pltpu.VMEM((5120,), BF16),
        pltpu.VMEM((16, 128), jnp.int32),
        pltpu.VMEM((4, CAP, 5 * HD), BF16),
        pltpu.VMEM((4, NY, NZ, 32, HD), BF16),
        pltpu.VMEM((2, NY, NZ, 32, HD), BF16),
        pltpu.VMEM((CAP, 5248), BF16),
        pltpu.VMEM((512, 256), BF16),
        pltpu.VMEM((16, 128), BF16),
        pltpu.VMEM((8, 16, 128), BF16),
        pltpu.VMEM((NZ, 16, 128), BF16),
        pltpu.VMEM((16, 128), F32),
        pltpu.VMEM((128, 128), F32),
        pltpu.VMEM((ROWS, ROWS), BF16),
        pltpu.VMEM((128, ROWS), BF16),
        pltpu.VMEM((16, ROWS), BF16),
        pltpu.VMEM((ROWS, 256), F32),
        pltpu.VMEM((ROWS, ROWS), BF16),
        pltpu.VMEM((ROWS, 128), BF16),
        pltpu.VMEM((128, ROWS), BF16),
        pltpu.VMEM((HD, ROWS), BF16),
        pltpu.VMEM((HD, ROWS), BF16),
        pltpu.VMEM((ROWS, HD), BF16),
        pltpu.VMEM((8, ROWS), F32),
        pltpu.VMEM((4, 128, HD), BF16),
        pltpu.VMEM((4, CAP, 5 * HD), BF16),
        pltpu.VMEM((NY, 8, 128), F32),
        pltpu.VMEM((20, 8, 128), F32),
        pltpu.VMEM((8, 256), F32),
        pltpu.VMEM((4, 8, 256), F32),
        dma((7,)), dma((4, 2)), dma((8,)), dma, dma, dma((4,)), dma((8,)),
        dma((2, 4, 9)), dma((2, 4, 9)), dma((2, 16)), dma((2, 16)), dma((2, 16)), dma((2, 4, 16)), dma, dma,
        dma((16,)), dma((2, 16)), dma((8,)), dma((5,)), dma((4, 4)), dma((20,)), dma((4, 2)), dma((4,)),
        pltpu.SemaphoreType.REGULAR,
    ]
    out, router = pl.pallas_call(
        kernel,
        out_shape=(
            jax.ShapeDtypeStruct((4, CAP, 5 * HD), BF16),
            jax.ShapeDtypeStruct((8, 128), F32),
        ),
        in_specs=[pl.BlockSpec(memory_space=pltpu.SMEM)] + [hbm] * 7,
        out_specs=(vmem,) * 2,
        scratch_shapes=scratch,
        compiler_params=pltpu.CompilerParams(
            collective_id=0, has_side_effects=True, vmem_limit_bytes=56 * 2**20
        ),
        name="routed_attention",
    )(
        chosen, owner.reshape(16, 128), router_weight,
        queries, keys, values, grad_out, stream,
    )

    def split(out_ref, router_in, *refs):
        for i in range(4):
            refs[i][...] = out_ref[i]
        refs[4][...] = router_in[0, :40]

    wide = jax.ShapeDtypeStruct((CAP, 5 * HD), BF16)
    return pl.pallas_call(
        split,
        out_shape=(wide, wide, wide, wide, jax.ShapeDtypeStruct((40,), F32)),
        in_specs=[vmem] * 2,
        out_specs=(vmem,) * 5,
        name="split_outputs",
    )(out, router)


def solution(mesh):
    return jax.shard_map(
        body,
        mesh=mesh,
        in_specs=(
            P("seq", None),
            P("seq", "head"),
            P("seq", "head"),
            P("seq", "head"),
            P(),
            P(),
            P(),
            P("seq", "head"),
        ),
        out_specs=(
            P("seq", "head"),
            P("seq", "head"),
            P("seq", "head"),
            P("seq", "head"),
            P("seq"),
        ),
        check_vma=False,
    )
```
